32 devices in a mesh: groups: 2 (over y), leaf: 4 (over z), sub: 4 (over x, core).
Axes of the slice: x: 2, y: 2, z: 4, core: 2. Of those that a mesh axis runs over, the one named last changes fastest.
Arguments:
- features: bfloat16 [512, 8192], P(('groups', 'leaf'), 'sub'), parts along dimension 0, may hold values from -6 to 6
- occupancy: int32 [512, 256], P(('groups', 'leaf'), 'sub'), parts along dimension 0, may hold values 0 or 1
- offsets: int32 [512, 13], P(('groups', 'leaf')), parts along dimension 0, may hold values from 1 to 64, as said below
- counts: int32 [512], P(('groups', 'leaf')), parts along dimension 0, may hold values from 1 to 13, as said below
- right_side: float32 [512, 256], P(('groups', 'leaf'), 'sub'), parts along dimension 0, may hold values from -3 to 8
Outputs:
- solution_field: float32 [512, 256], P(('groups', 'leaf'), 'sub'), parts along dimension 0
- residual: float32 [512, 256], P(('groups', 'leaf'), 'sub'), parts along dimension 0
The draws below stay inside these ranges and needn't reach their ends.
There are 2 independent parts, one for each index of `groups`. The reference program is written for one: setup_inputs(seed, part) draws one part's arguments, and reference() takes and returns one part's arrays. A program takes and returns all parts, laid end to end along the dimension named above; each array names one. Nothing has to cross between parts.
Inputs may be any that keep to these rules, and one draw needn't show every extreme that they name: `offsets`: every offset is at least 1 and at most 64; some offset equals 64. `counts`: some leaf uses all 13 slots and some leaf uses one.
All inputs are finite; a program needn't handle non-finite values. No bound on the sum of `occupancy` on one device may be relied on, other than what follows from the above.
Results may differ from the reference program's by a relative error of at most 0.0003.
Values may be sent and summed in bfloat16 or wider, within the bound.
A program may use at most 192 MiB of HBM per device.

```python
import jax
import jax.numpy as jnp
from jax import lax

VOX = 256
FEAT = 32
NBR = 13
ITERS = 3
LEAF_DEV = 64
LEAVES = 256


def draw_offsets(key, part):
    key = jax.random.fold_in(key, 11)
    key_one, key_two = jax.random.split(key)
    offset_draw = jax.random.randint(key_one, (LEAVES, NBR), 1, LEAF_DEV + 1)
    chosen = jax.random.randint(key_two, (), 0, LEAVES)
    return offset_draw.at[chosen, 0].set(LEAF_DEV).astype(jnp.int32)


def draw_counts(key, part):
    key = jax.random.fold_in(key, 23)
    key_one, key_two, key_three = jax.random.split(key, 3)
    lower = jax.random.randint(key_one, (LEAVES,), 0, NBR)
    upper = jax.random.randint(key_two, (LEAVES,), 0, NBR)
    counted = 1 + jnp.minimum(lower, upper)
    chosen = jax.random.randint(key_three, (2,), 0, LEAVES // 2)
    counted = counted.at[chosen[0]].set(NBR)
    counted = counted.at[chosen[1] + LEAVES // 2].set(1)
    return counted.astype(jnp.int32)


def draw_features(key, part):
    key = jax.random.fold_in(key, 31)
    values = 2.0 * jax.random.normal(key, (LEAVES, FEAT * VOX), jnp.float32)
    return jnp.clip(values, -6.0, 6.0).astype(jnp.bfloat16)


def draw_right_side(key, part):
    key = jax.random.fold_in(key, 47)
    key_one, key_two = jax.random.split(key)
    position = jnp.arange(LEAVES, dtype=jnp.float32)[:, None] / LEAVES
    level = jax.random.uniform(key_one, (LEAVES, 1), jnp.float32, 0.7, 1.4)
    level = level * (1.0 + 2.0 * position)
    noise = jnp.clip(jax.random.normal(key_two, (LEAVES, VOX), jnp.float32), -3.0, 3.0)
    return (level + noise).astype(jnp.float32)


def touch_ends(entries, key, low, high):
    dims = entries.shape
    index_at = [jax.random.randint(jax.random.fold_in(key, axis), (), 0, dims[axis]) for axis in range(len(dims))]
    entries = entries.at[tuple(index_at)].set(low)
    longest = dims.index(max(dims))
    index_at[longest] = (index_at[longest] + 1) % dims[longest]
    return entries.at[tuple(index_at)].set(high)


def setup_inputs(seed: int = 0, part: int = 0) -> dict:
    arg_keys = jax.random.split(jax.random.key(seed), 6)
    own_keys = jax.random.split(jax.random.fold_in(arg_keys[5], part), 6)
    features = draw_features(jax.random.fold_in(jax.random.fold_in(arg_keys[5], part), 71), part)
    occupancy = touch_ends((jax.random.randint(own_keys[1], (LEAVES, VOX), 0, 3) < 2).astype(jnp.int32), jax.random.fold_in(own_keys[1], 1), 0, 1)
    offsets = draw_offsets(jax.random.fold_in(jax.random.fold_in(arg_keys[5], part), 71), part)
    counts = draw_counts(jax.random.fold_in(jax.random.fold_in(arg_keys[5], part), 71), part)
    right_side = draw_right_side(jax.random.fold_in(jax.random.fold_in(arg_keys[5], part), 71), part)
    return dict(features=features, occupancy=occupancy, offsets=offsets, counts=counts, right_side=right_side)


diag_shift = 0.25


def slot_table(offsets, counts):
    leaves = offsets.shape[0]
    anchor = jnp.arange(leaves, dtype=jnp.int32)[:, None]
    target = anchor + offsets
    slot_idx = jnp.arange(offsets.shape[1], dtype=jnp.int32)[None, :]
    usable = (slot_idx < counts[:, None]) & (target < leaves)
    target = jnp.where(usable, target, anchor)
    targets = jnp.concatenate([anchor, target], axis=1)
    weights = jnp.concatenate([jnp.ones((leaves, 1), jnp.float32), usable.astype(jnp.float32)], axis=1)
    return targets, weights


def apply_blocks(features, squares, targets, weights, vectors):
    def per_leaf(leaf_at):
        target = targets[leaf_at]
        columns = features[target].astype(jnp.float32)
        row_feat = features[leaf_at].astype(jnp.float32)
        inner = jnp.einsum('ca,scb->sab', row_feat, columns, precision=lax.Precision.HIGHEST)
        distance = squares[leaf_at][None, :, None] + squares[target][:, None, :] - 2.0 * inner
        kernel = jnp.exp(-distance / (2.0 * FEAT)) * weights[leaf_at][:, None, None]
        picked = vectors[:, target]
        forward = jnp.einsum('sab,nsb->na', kernel, picked, precision=lax.Precision.HIGHEST)
        mirror = jnp.einsum('sab,na->snb', kernel[1:], vectors[:, leaf_at], precision=lax.Precision.HIGHEST)
        return forward, mirror

    forward, mirror = lax.map(per_leaf, jnp.arange(LEAVES, dtype=jnp.int32))
    flat = mirror.reshape((LEAVES * NBR,) + mirror.shape[2:])
    mirrored = jax.ops.segment_sum(flat, targets[:, 1:].reshape(-1), num_segments=LEAVES)
    return forward + mirrored


def reference(features, occupancy, offsets, counts, right_side):
    features = features.reshape((LEAVES, FEAT, VOX))
    squares = jnp.sum(jnp.square(features.astype(jnp.float32)), axis=1)
    targets, weights = slot_table(offsets, counts)
    occupied = occupancy.astype(jnp.float32)
    vectors = jnp.stack([jnp.ones_like(right_side), occupied * right_side])
    first = apply_blocks(features, squares, targets, weights, vectors)
    diagonal = diag_shift + first[:, 0] / VOX
    image_vec = diagonal * right_side + occupied * first[:, 1] / VOX

    def operate(field):
        coupled = apply_blocks(features, squares, targets, weights, (occupied * field)[None])
        return diagonal * field + occupied * coupled[:, 0] / VOX

    solution_field = jnp.zeros_like(right_side)
    residual, direction = right_side, right_side
    norm_now = jnp.sum(residual * residual)
    for iteration in range(ITERS):
        if iteration > 0:
            image_vec = operate(direction)
        step_size = norm_now / jnp.sum(direction * image_vec)
        solution_field = solution_field + step_size * direction
        residual = residual - step_size * image_vec
        norm_next = jnp.sum(residual * residual)
        direction = residual + (norm_next / norm_now) * direction
        norm_now = norm_next
    return solution_field, residual
```

```python
import functools

import jax
import jax.numpy as jnp
from jax import lax
from jax.experimental import pallas as pl
from jax.experimental.pallas import tpu as pltpu
from jax.sharding import PartitionSpec as P

ITERS = 3
GROUP = 4
LANES = 128
VMEM_LIMIT = 48 * 1024 * 1024
diag_shift = 0.25
MESH = pl.DeviceIdType.MESH


def shifted(x, axis, by):
    peers = lax.axis_size(axis)
    pairs = [(i, i + by) for i in range(peers) if 0 <= i + by < peers]
    return lax.ppermute(x, axis, pairs)


def apply_kernel(with_ones, rows_at, cols_at, mirror_at, groups_ref, row_ref, col_ref, u_ref, v_ref,
                 fwd_ref, mir_ref, u_wide, fwd_acc, mir_acc):
    leaves, share = u_ref.shape
    voxels = v_ref.shape[1]
    u_wide[...] = jnp.broadcast_to(u_ref[...][:, :, None], u_wide.shape)
    fwd_acc[...] = jnp.zeros_like(fwd_acc)
    mir_acc[...] = jnp.zeros_like(mir_acc)

    def fold_lanes(x):
        return sum(x[:, i:i + LANES] for i in range(0, voxels, LANES))

    def fold_rows(x):
        return sum(x[i:i + 8, :] for i in range(0, share, 8))

    def group(g, carry):
        for i in range(GROUP):
            at = g * GROUP + i
            row = rows_at[at]
            col = cols_at[at]
            mir = mirror_at[at]
            row_read = jnp.minimum(row, leaves - 1)
            block = jnp.exp(
                jnp.dot(row_ref[row_read], col_ref[col], preferred_element_type=jnp.float32)
            )
            v_row = v_ref[pl.ds(col, 1), :]
            wide = u_wide[row_read]
            wide = jnp.concatenate([wide] * (voxels // LANES), axis=1)
            fwd_acc[0, row] += fold_lanes(block * v_row)
            mir_acc[0, mir] += fold_rows(block * wide)
            if with_ones:
                fwd_acc[1, row] += fold_lanes(block)
                mir_acc[1, mir] += fold_rows(block)
        return carry

    lax.fori_loop(0, groups_ref[0], group, 0)
    for n in range(fwd_ref.shape[0]):
        fwd_ref[n] = jnp.sum(fwd_acc[n, :leaves], axis=-1)
        mir_ref[n] = jnp.sum(mir_acc[n, :2 * leaves], axis=1)


def apply_blocks(with_ones, lists, row_feat, col_feat, u, v):
    leaves, share = u.shape
    voxels = v.shape[1]
    count = 2 if with_ones else 1
    smem = pl.BlockSpec(memory_space=pltpu.SMEM)
    vmem = pl.BlockSpec(memory_space=pltpu.VMEM)
    return pl.pallas_call(
        functools.partial(apply_kernel, with_ones),
        out_shape=(
            jax.ShapeDtypeStruct((count, leaves, share), jnp.float32),
            jax.ShapeDtypeStruct((count, 2 * leaves, voxels), jnp.float32),
        ),
        in_specs=[smem] * 4 + [vmem] * 4,
        out_specs=(vmem, vmem),
        scratch_shapes=[
            pltpu.VMEM((leaves, share, LANES), jnp.float32),
            pltpu.VMEM((count, leaves + 1, share, LANES), jnp.float32),
            pltpu.VMEM((count, 2 * leaves + 1, 8, voxels), jnp.float32),
        ],
        compiler_params=pltpu.CompilerParams(vmem_limit_bytes=VMEM_LIMIT),
    )(*lists, row_feat, col_feat, u, v)


def update_kernel(first, last, n_leaf, n_sub, *refs):
    refs = list(refs)
    fwd_ref, mir_ref, occ_ref, dir_ref = refs[:4]
    del refs[:4]
    if first:
        window_ref = refs.pop(0)
        out_refs = refs[:7]
        del refs[:7]
        x_out, res_out, dir_out, u_out, win_dir_out, win_res_out, diag_out = out_refs
    else:
        diag_ref, x_ref, res_ref = refs[:3]
        del refs[:3]
        if last:
            x_out, res_out = refs[:2]
            del refs[:2]
        else:
            win_dir_ref, win_res_ref = refs[:2]
            x_out, res_out, dir_out, u_out, win_dir_out, win_res_out = refs[2:8]
            del refs[:8]
    mir_send, mir_own, mir_back, img_own, img_ahead, scalars, send_sem, recv_sem = refs

    group_at = lax.axis_index("groups")
    leaf_at = lax.axis_index("leaf")
    sub_at = lax.axis_index("sub")
    devices = n_leaf * n_sub
    leaves, share = dir_ref.shape
    voxels = share * n_sub

    def peer(leaf_by, sub_by):
        return (
            group_at,
            lax.rem(leaf_at + leaf_by, n_leaf),
            lax.rem(sub_at + sub_by, n_sub),
        )

    barrier = pltpu.get_barrier_semaphore()

    def greet(k, carry):
        pl.semaphore_signal(barrier, inc=1, device_id=peer(k // n_sub, k % n_sub), device_id_type=MESH)
        return carry

    lax.fori_loop(1, devices, greet, 0)
    for s in range(n_sub):
        mir_send[s] = mir_ref[:, :, s * share:(s + 1) * share]
    pl.semaphore_wait(barrier, devices - 1)

    def copy(src, dst, sem, leaf_by, sub_by):
        return pltpu.make_async_remote_copy(
            src_ref=src, dst_ref=dst, send_sem=send_sem.at[sem], recv_sem=recv_sem.at[sem],
            device_id=peer(leaf_by, sub_by), device_id_type=MESH,
        )

    copies = []
    for s in range(n_sub):
        to = lax.rem(sub_at + s, n_sub)
        copies.append(copy(mir_send.at[to, :, leaves:], mir_back.at[s], s, 1, s))
        copies[-1].start()
    for s in range(1, n_sub):
        to = lax.rem(sub_at + s, n_sub)
        copies.append(copy(mir_send.at[to, :, :leaves], mir_own.at[s], n_sub + s, 0, s))
        copies[-1].start()
    total = fwd_ref[...] + mir_send[sub_at, :, :leaves]
    for c in copies:
        c.wait()
    for s in range(1, n_sub):
        total += mir_own[s]
    for s in range(n_sub):
        total += mir_back[s]
    occ = occ_ref[...]
    direction = dir_ref[...]
    if first:
        diagonal = diag_shift + total[1] / voxels
        residual = direction
        field = jnp.zeros_like(direction)
        diag_out[...] = diagonal
    else:
        diagonal = diag_ref[...]
        residual = res_ref[...]
        field = x_ref[...]
    image = diagonal * direction + occ * total[0] / voxels
    sums = (residual * residual, direction * image, residual * image, image * image)
    sub_iota = lax.broadcasted_iota(jnp.int32, (8, LANES), 0)
    packed = jnp.zeros((8, LANES), jnp.float32)
    for i, term in enumerate(sums):
        packed = jnp.where(sub_iota == i, jnp.sum(term), packed)
    scalars[0] = packed

    def tell(k, carry):
        copy(scalars.at[0], scalars.at[k], 4 * n_sub, k // n_sub, k % n_sub).start()
        return carry

    lax.fori_loop(1, devices, tell, 0)
    copies = []
    if not last:
        img_own[0] = occ * image
        for s in range(n_sub):
            copies.append(copy(img_own.at[0], img_ahead.at[s], 2 * n_sub + s, n_leaf - 1, s))
            copies[-1].start()
        for s in range(1, n_sub):
            copies.append(copy(img_own.at[0], img_own.at[s], 3 * n_sub + s, 0, s))
            copies[-1].start()
    everyone = copy(scalars.at[1:], scalars.at[1:], 4 * n_sub, 1, 0)
    everyone.wait()
    sums = jnp.sum(scalars[...], axis=0)
    rr = sums[0:1, :]
    step = rr / sums[1:2, :]
    new = rr - 2.0 * step * sums[2:3, :] + step * step * sums[3:4, :]
    beta = new / rr
    step_own = step[:, :share]
    beta_own = beta[:, :share]
    x_out[...] = field + step_own * direction
    residual = residual - step_own * image
    res_out[...] = residual
    if last:
        return
    direction = residual + beta_own * direction
    dir_out[...] = direction
    u_out[...] = occ * direction
    for c in copies:
        c.wait()
    if first:
        win_dir_ref = win_res_ref = window_ref
    step_wide = step[:, :1]
    beta_wide = beta[:, :1]
    for part, held in enumerate((img_own, img_ahead)):
        image_window = jnp.concatenate(
            [held[lax.rem(sub_at - s + n_sub, n_sub)] for s in range(n_sub)], axis=1
        )
        rows = slice(part * leaves, (part + 1) * leaves)
        res_window = win_res_ref[rows, :] - step_wide * image_window
        win_res_out[rows, :] = res_window
        win_dir_out[rows, :] = res_window + beta_wide * win_dir_ref[rows, :]


def update(first, last, collective_id, args):
    n_leaf, n_sub = lax.axis_size("leaf"), lax.axis_size("sub")
    count = 2 if first else 1
    leaves, share = args[3].shape
    voxels = share * n_sub
    own = jax.ShapeDtypeStruct((leaves, share), jnp.float32)
    window = jax.ShapeDtypeStruct((2 * leaves, voxels), jnp.float32)
    out_shape = (own, own) if last else (own, own, own, own, window, window)
    if first:
        out_shape = out_shape + (own,)
    vmem = pl.BlockSpec(memory_space=pltpu.VMEM)
    return pl.pallas_call(
        functools.partial(update_kernel, first, last, n_leaf, n_sub),
        out_shape=out_shape,
        in_specs=[vmem] * len(args),
        out_specs=(vmem,) * len(out_shape),
        scratch_shapes=[
            pltpu.VMEM((n_sub, count, 2 * leaves, share), jnp.float32),
            pltpu.VMEM((n_sub, count, leaves, share), jnp.float32),
            pltpu.VMEM((n_sub, count, leaves, share), jnp.float32),
            pltpu.VMEM((n_sub, leaves, share), jnp.float32),
            pltpu.VMEM((n_sub, leaves, share), jnp.float32),
            pltpu.VMEM((n_leaf * n_sub, 8, LANES), jnp.float32),
            pltpu.SemaphoreType.DMA((4 * n_sub + 1,)),
            pltpu.SemaphoreType.DMA((4 * n_sub + 1,)),
        ],
        compiler_params=pltpu.CompilerParams(
            collective_id=collective_id, has_side_effects=True, vmem_limit_bytes=VMEM_LIMIT
        ),
    )(*args)


def three_parts(x):
    parts = []
    for _ in range(3):
        part = lax.reduce_precision(x, 8, 7)
        parts.append(part.astype(jnp.bfloat16))
        x = x - part
    return parts


def block_lists(offsets, counts):
    leaves, slots = offsets.shape
    total_leaves = leaves * lax.axis_size("leaf")
    anchor = jnp.arange(leaves, dtype=jnp.int32)[:, None]
    target = anchor + offsets
    slot_idx = jnp.arange(slots, dtype=jnp.int32)[None, :]
    usable = (slot_idx < counts[:, None]) & (target + lax.axis_index("leaf") * leaves < total_leaves)
    used = jnp.concatenate([jnp.ones((leaves, 1), bool), usable], axis=1).reshape(-1)
    cols = jnp.concatenate([anchor, target], axis=1).reshape(-1)
    rows = jnp.broadcast_to(anchor, (leaves, slots + 1)).reshape(-1)
    mirrors = jnp.concatenate([jnp.full((leaves, 1), 2 * leaves, jnp.int32), target], axis=1).reshape(-1)
    size = rows.shape[0]
    idx = jnp.arange(size, dtype=jnp.int32)
    used_i = used.astype(jnp.int32)
    before = jnp.sum(jnp.where(idx[None, :] < idx[:, None], used_i[None, :], 0), axis=1)
    length = -(-size // GROUP) * GROUP
    place = jnp.arange(length, dtype=jnp.int32)
    hit = (before[None, :] == place[:, None]) & used[None, :]
    any_hit = jnp.sum(hit.astype(jnp.int32), axis=1)

    def compact(values, fill):
        return jnp.sum(jnp.where(hit, values[None, :], 0), axis=1) + (1 - any_hit) * fill

    count = jnp.sum(used_i)
    return (
        compact(rows, leaves),
        compact(cols, 0),
        compact(mirrors, 2 * leaves),
        ((count + GROUP - 1) // GROUP).reshape((1,)),
    )


def body(features, occupancy, offsets, counts, right_side):
    leaves, share = right_side.shape
    n_sub = lax.axis_size("sub")
    voxels = share * n_sub
    feat = features.shape[1] * n_sub // voxels
    occ = occupancy.astype(jnp.float32)
    masked = occ * right_side
    ahead_part = shifted(features, "leaf", -1)
    ahead_masked = shifted(masked, "leaf", -1)
    owned_flat = lax.all_gather(features, "sub", axis=1, tiled=True)
    ahead_flat = lax.all_gather(ahead_part, "sub", axis=1, tiled=True)
    window = lax.all_gather(
        jnp.concatenate([masked, ahead_masked], axis=0), "sub", axis=1, tiled=True
    )
    lists = block_lists(offsets, counts)

    owned = owned_flat.reshape((leaves, feat, voxels))
    ahead = ahead_flat.reshape((leaves, feat, voxels))
    cols = jnp.concatenate([owned, ahead], axis=0)
    scale = 1.0 / (2.0 * feat)
    neg_sq = -scale * jnp.sum(jnp.square(cols.astype(jnp.float32)), axis=1)
    parts = three_parts(neg_sq)
    depth = -(-(feat + 6) // 16) * 16
    ones_c = jnp.ones((2 * leaves, 3, voxels), jnp.bfloat16)
    pad_c = jnp.zeros((2 * leaves, depth - feat - 6, voxels), jnp.bfloat16)
    col_feat = jnp.concatenate(
        [cols] + [p[:, None, :] for p in parts] + [ones_c, pad_c], axis=1
    )
    start = lax.axis_index("sub") * share
    own_rows = lax.dynamic_slice_in_dim(owned, start, share, 2)
    own_parts = [lax.dynamic_slice_in_dim(p[:leaves], start, share, 1)[:, None, :] for p in parts]
    row_feat = jnp.concatenate(
        [own_rows * jnp.bfloat16(2.0 * scale), jnp.ones((leaves, 3, share), jnp.bfloat16)]
        + own_parts
        + [jnp.zeros((leaves, depth - feat - 6, share), jnp.bfloat16)],
        axis=1,
    ).transpose((0, 2, 1))

    fwd, mir = apply_blocks(True, lists, row_feat, col_feat, masked, window)
    x, res, direction, u, win_dir, win_res, diagonal = update(
        True, False, 0, (fwd, mir, occ, right_side, window)
    )
    for it in range(1, ITERS):
        fwd, mir = apply_blocks(False, lists, row_feat, col_feat, u, win_dir)
        args = (fwd, mir, occ, direction, diagonal, x, res)
        if it == ITERS - 1:
            x, res = update(False, True, it, args)
        else:
            x, res, direction, u, win_dir, win_res = update(
                False, False, it, args + (win_dir, win_res)
            )
    return x, res


def solution(mesh):
    in_specs = (
        P(("groups", "leaf"), "sub"),
        P(("groups", "leaf"), "sub"),
        P(("groups", "leaf"), None),
        P(("groups", "leaf")),
        P(("groups", "leaf"), "sub"),
    )
    out_specs = (P(("groups", "leaf"), "sub"), P(("groups", "leaf"), "sub"))
    return jax.shard_map(body, mesh=mesh, in_specs=in_specs, out_specs=out_specs, check_vma=False)
```

```python
import functools

import jax
import jax.numpy as jnp
from jax import lax
from jax.experimental import pallas as pl
from jax.experimental.pallas import tpu as pltpu
from jax.sharding import PartitionSpec as P

ITERS = 3
GROUP = 4
LANES = 128
VMEM_LIMIT = 48 * 1024 * 1024
diag_shift = 0.25
MESH = pl.DeviceIdType.MESH


def apply_kernel(with_ones, rows_at, cols_at, mirror_at, groups_ref, row_ref, col_ref, row_w_ref, col_w_ref, u_ref, v_ref,
                 fwd_ref, mir_ref, u_wide, v_scaled, fwd_acc, mir_acc):
    leaves, share = u_ref.shape
    voxels = v_ref.shape[1]
    count = fwd_ref.shape[0]
    row_w = row_w_ref[...]
    col_w = col_w_ref[...]
    u_wide[0] = jnp.broadcast_to((u_ref[...] * row_w)[:, :, None], u_wide.shape[1:])
    v_scaled[0] = v_ref[...] * col_w
    if with_ones:
        u_wide[1] = jnp.broadcast_to(row_w[:, :, None], u_wide.shape[1:])
        v_scaled[1] = col_w
    fwd_acc[...] = jnp.zeros_like(fwd_acc)
    mir_acc[...] = jnp.zeros_like(mir_acc)

    def fold_lanes(x):
        return sum(x[:, i:i + LANES] for i in range(0, voxels, LANES))

    def fold_rows(x):
        return sum(x[i:i + 8, :] for i in range(0, share, 8))

    def group(g, carry):
        marks, blocks = [], []
        for i in range(GROUP):
            at = g * GROUP + i
            marks.append((rows_at[at], cols_at[at], mirror_at[at]))
        for row, col, mir in marks:
            blocks.append(jnp.exp(jnp.dot(
                row_ref[jnp.minimum(row, leaves - 1)], col_ref[col],
                preferred_element_type=jnp.float32,
            )))
        for (row, col, mir), block in zip(marks, blocks):
            row_read = jnp.minimum(row, leaves - 1)
            for n in range(count):
                wide = jnp.concatenate([u_wide[n, row_read]] * (voxels // LANES), axis=1)
                fwd_acc[n, row] += fold_lanes(block * v_scaled[n, pl.ds(col, 1), :])
                mir_acc[n, mir] += fold_rows(block * wide)
        return carry

    lax.fori_loop(0, groups_ref[0], group, 0)
    for n in range(count):
        fwd_ref[n] = jnp.sum(fwd_acc[n, :leaves], axis=-1) * row_w
        mir_ref[n] = jnp.sum(mir_acc[n, :2 * leaves], axis=1) * col_w


def apply_blocks(with_ones, lists, feats, u, v):
    leaves, share = u.shape
    voxels = v.shape[1]
    count = 2 if with_ones else 1
    smem = pl.BlockSpec(memory_space=pltpu.SMEM)
    vmem = pl.BlockSpec(memory_space=pltpu.VMEM)
    return pl.pallas_call(
        functools.partial(apply_kernel, with_ones),
        out_shape=(
            jax.ShapeDtypeStruct((count, leaves, share), jnp.float32),
            jax.ShapeDtypeStruct((count, 2 * leaves, voxels), jnp.float32),
        ),
        in_specs=[smem] * 4 + [vmem] * 6,
        out_specs=(vmem, vmem),
        scratch_shapes=[
            pltpu.VMEM((count, leaves, share, LANES), jnp.float32),
            pltpu.VMEM((count, 2 * leaves, voxels), jnp.float32),
            pltpu.VMEM((count, leaves + 1, share, LANES), jnp.float32),
            pltpu.VMEM((count, 2 * leaves + 1, 8, voxels), jnp.float32),
        ],
        compiler_params=pltpu.CompilerParams(vmem_limit_bytes=VMEM_LIMIT),
    )(*lists, *feats, u, v)


def gather_kernel(n_leaf, n_sub, slab_ref, field_ref, own_out, ahead_out, window_out,
                  field_own, field_ahead, send_sem, recv_sem, field_send, field_recv):
    group_at = lax.axis_index("groups")
    leaf_at = lax.axis_index("leaf")
    sub_at = lax.axis_index("sub")
    inner = 2 if n_sub % 2 == 0 else 1
    n_out = n_sub // inner
    out_at = sub_at // inner
    in_at = sub_at % inner
    leaves = field_ref.shape[0]
    behind = lax.rem(leaf_at + n_leaf - 1, n_leaf)
    devices = n_leaf * n_sub

    barrier = pltpu.get_barrier_semaphore()

    def greet(k, carry):
        to = (
            group_at,
            lax.rem(leaf_at + k // n_sub, n_leaf),
            lax.rem(sub_at + k % n_sub, n_sub),
        )
        pl.semaphore_signal(barrier, inc=1, device_id=to, device_id_type=MESH)
        return carry

    lax.fori_loop(1, devices, greet, 0)
    field_own[0] = field_ref[...]
    pl.semaphore_wait(barrier, devices - 1)

    sent = []

    def send(src, dst, slot, leaf, sub):
        c = pltpu.make_async_remote_copy(
            src_ref=src, dst_ref=dst, send_sem=send_sem.at[len(sent)], recv_sem=recv_sem.at[slot],
            device_id=(group_at, leaf, sub), device_id_type=MESH,
        )
        c.start()
        sent.append(c)

    def arrived(dst, slot):
        pltpu.make_async_remote_copy(
            src_ref=slab_ref, dst_ref=dst, send_sem=send_sem.at[0], recv_sem=recv_sem.at[slot],
            device_id=(group_at, leaf_at, sub_at), device_id_type=MESH,
        ).wait_recv()

    def sub_of(outer_by, other):
        return lax.rem(out_at + outer_by, n_out) * inner + (inner - 1 - in_at if other else in_at)

    partner = sub_of(0, True)
    send(slab_ref, ahead_out.at[sub_at], n_sub + sub_at, behind, sub_at)
    for d in range(1, n_out):
        send(slab_ref, own_out.at[sub_at], sub_at, leaf_at, sub_of(d, False))
    if inner == 2:
        send(slab_ref, own_out.at[sub_at], sub_at, leaf_at, partner)
    field_copies = []
    for s in range(n_sub):
        to = lax.rem(sub_at + s, n_sub)
        field_copies.append(pltpu.make_async_remote_copy(
            src_ref=field_ref, dst_ref=field_ahead.at[s],
            send_sem=field_send.at[s], recv_sem=field_recv.at[s],
            device_id=(group_at, behind, to), device_id_type=MESH,
        ))
        if s:
            field_copies.append(pltpu.make_async_remote_copy(
                src_ref=field_ref, dst_ref=field_own.at[s],
                send_sem=field_send.at[n_sub + s], recv_sem=field_recv.at[n_sub + s],
                device_id=(group_at, leaf_at, to), device_id_type=MESH,
            ))
    for c in field_copies:
        c.start()
    own_out[sub_at] = slab_ref[...]
    arrived(ahead_out.at[sub_at], n_sub + sub_at)
    for d in range(1, n_out):
        send(ahead_out.at[sub_at], ahead_out.at[sub_at], n_sub + sub_at, leaf_at, sub_of(d, False))
    if inner == 2:
        send(ahead_out.at[sub_at], ahead_out.at[sub_at], n_sub + sub_at, leaf_at, partner)
    for base, out in ((0, own_out), (n_sub, ahead_out)):
        for d in range(1, n_out):
            slot = sub_of(n_out - d, False)
            arrived(out.at[slot], base + slot)
            if inner == 2:
                send(out.at[slot], out.at[slot], base + slot, leaf_at, partner)
    for c in field_copies:
        c.wait()
    for part, held in enumerate((field_own, field_ahead)):
        window_out[part * leaves:(part + 1) * leaves, :] = jnp.concatenate(
            [held[lax.rem(sub_at - s + n_sub, n_sub)] for s in range(n_sub)], axis=1
        )
    if inner == 2:
        for base, out in ((0, own_out), (n_sub, ahead_out)):
            for d in range(n_out):
                slot = sub_of(n_out - d, True)
                arrived(out.at[slot], base + slot)
    for c in sent:
        c.wait_send()


def gather_all(slab, field):
    n_leaf, n_sub = lax.axis_size("leaf"), lax.axis_size("sub")
    leaves, share = field.shape
    vmem = pl.BlockSpec(memory_space=pltpu.VMEM)
    slabs = jax.ShapeDtypeStruct((n_sub,) + slab.shape, slab.dtype)
    return pl.pallas_call(
        functools.partial(gather_kernel, n_leaf, n_sub),
        out_shape=(slabs, slabs, jax.ShapeDtypeStruct((2 * leaves, share * n_sub), jnp.float32)),
        in_specs=[vmem] * 2,
        out_specs=(vmem,) * 3,
        scratch_shapes=[
            pltpu.VMEM((n_sub, leaves, share), jnp.float32),
            pltpu.VMEM((n_sub, leaves, share), jnp.float32),
            pltpu.SemaphoreType.DMA((3 * n_sub + 2,)),
            pltpu.SemaphoreType.DMA((2 * n_sub,)),
            pltpu.SemaphoreType.DMA((2 * n_sub,)),
            pltpu.SemaphoreType.DMA((2 * n_sub,)),
        ],
        compiler_params=pltpu.CompilerParams(
            collective_id=ITERS, has_side_effects=True, vmem_limit_bytes=VMEM_LIMIT
        ),
    )(slab, field)


def update_kernel(first, last, n_leaf, n_sub, *refs):
    refs = list(refs)
    fwd_ref, mir_ref, occ_ref, dir_ref = refs[:4]
    del refs[:4]
    if first:
        window_ref = refs.pop(0)
        out_refs = refs[:7]
        del refs[:7]
        x_out, res_out, dir_out, u_out, win_dir_out, win_res_out, diag_out = out_refs
    else:
        diag_ref, x_ref, res_ref = refs[:3]
        del refs[:3]
        if last:
            x_out, res_out = refs[:2]
            del refs[:2]
        else:
            win_dir_ref, win_res_ref = refs[:2]
            x_out, res_out, dir_out, u_out, win_dir_out, win_res_out = refs[2:8]
            del refs[:8]
    mir_send, mir_own, mir_back, img_own, img_ahead, scalars, send_sem, recv_sem = refs

    group_at = lax.axis_index("groups")
    leaf_at = lax.axis_index("leaf")
    sub_at = lax.axis_index("sub")
    devices = n_leaf * n_sub
    leaves, share = dir_ref.shape
    voxels = share * n_sub

    def peer(leaf_by, sub_by):
        return (
            group_at,
            lax.rem(leaf_at + leaf_by, n_leaf),
            lax.rem(sub_at + sub_by, n_sub),
        )

    barrier = pltpu.get_barrier_semaphore()

    def greet(k, carry):
        pl.semaphore_signal(barrier, inc=1, device_id=peer(k // n_sub, k % n_sub), device_id_type=MESH)
        return carry

    lax.fori_loop(1, devices, greet, 0)
    for s in range(n_sub):
        mir_send[s] = mir_ref[:, :, s * share:(s + 1) * share]
    pl.semaphore_wait(barrier, devices - 1)

    def copy(src, dst, sem, leaf_by, sub_by):
        return pltpu.make_async_remote_copy(
            src_ref=src, dst_ref=dst, send_sem=send_sem.at[sem], recv_sem=recv_sem.at[sem],
            device_id=peer(leaf_by, sub_by), device_id_type=MESH,
        )

    copies = []
    for s in range(n_sub):
        to = lax.rem(sub_at + s, n_sub)
        copies.append(copy(mir_send.at[to, :, leaves:], mir_back.at[s], s, 1, s))
        copies[-1].start()
    for s in range(1, n_sub):
        to = lax.rem(sub_at + s, n_sub)
        copies.append(copy(mir_send.at[to, :, :leaves], mir_own.at[s], n_sub + s, 0, s))
        copies[-1].start()
    total = fwd_ref[...] + mir_send[sub_at, :, :leaves]
    for c in copies:
        c.wait()
    for s in range(1, n_sub):
        total += mir_own[s]
    for s in range(n_sub):
        total += mir_back[s]
    occ = occ_ref[...]
    direction = dir_ref[...]
    if first:
        diagonal = diag_shift + total[1] / voxels
        residual = direction
        field = jnp.zeros_like(direction)
        diag_out[...] = diagonal
    else:
        diagonal = diag_ref[...]
        residual = res_ref[...]
        field = x_ref[...]
    image = diagonal * direction + occ * total[0] / voxels
    sums = (residual * residual, direction * image, residual * image, image * image)
    lane = lax.broadcasted_iota(jnp.int32, (1, LANES), 1)
    packed = jnp.zeros((1, LANES), jnp.float32)
    for i, term in enumerate(sums):
        packed = jnp.where(lane == i, jnp.sum(term), packed)
    scalars[0] = packed

    def tell(k, carry):
        copy(scalars.at[0], scalars.at[k], 4 * n_sub, k // n_sub, k % n_sub).start()
        return carry

    lax.fori_loop(1, devices, tell, 0)
    copies = []
    if not last:
        img_own[0] = occ * image
        for s in range(n_sub):
            copies.append(copy(img_own.at[0], img_ahead.at[s], 2 * n_sub + s, n_leaf - 1, s))
            copies[-1].start()
        for s in range(1, n_sub):
            copies.append(copy(img_own.at[0], img_own.at[s], 3 * n_sub + s, 0, s))
            copies[-1].start()
    everyone = copy(scalars.at[1:], scalars.at[1:], 4 * n_sub, 1, 0)
    everyone.wait()
    sums = jnp.sum(scalars[...], axis=0)
    rr, dq, rq, qq = [
        jnp.sum(jnp.where(lane == i, sums, 0.0), axis=1, keepdims=True) for i in range(4)
    ]
    step = rr / dq
    new = rr - 2.0 * step * rq + step * step * qq
    beta = new / rr
    x_out[...] = field + step * direction
    residual = residual - step * image
    res_out[...] = residual
    if last:
        return
    direction = residual + beta * direction
    dir_out[...] = direction
    u_out[...] = occ * direction
    for c in copies:
        c.wait()
    if first:
        win_dir_ref = win_res_ref = window_ref
    for part, held in enumerate((img_own, img_ahead)):
        image_window = jnp.concatenate(
            [held[lax.rem(sub_at - s + n_sub, n_sub)] for s in range(n_sub)], axis=1
        )
        rows = slice(part * leaves, (part + 1) * leaves)
        res_window = win_res_ref[rows, :] - step * image_window
        win_res_out[rows, :] = res_window
        win_dir_out[rows, :] = res_window + beta * win_dir_ref[rows, :]


def update(first, last, collective_id, args):
    n_leaf, n_sub = lax.axis_size("leaf"), lax.axis_size("sub")
    count = 2 if first else 1
    leaves, share = args[3].shape
    voxels = share * n_sub
    own = jax.ShapeDtypeStruct((leaves, share), jnp.float32)
    window = jax.ShapeDtypeStruct((2 * leaves, voxels), jnp.float32)
    out_shape = (own, own) if last else (own, own, own, own, window, window)
    if first:
        out_shape = out_shape + (own,)
    vmem = pl.BlockSpec(memory_space=pltpu.VMEM)
    return pl.pallas_call(
        functools.partial(update_kernel, first, last, n_leaf, n_sub),
        out_shape=out_shape,
        in_specs=[vmem] * len(args),
        out_specs=(vmem,) * len(out_shape),
        scratch_shapes=[
            pltpu.VMEM((n_sub, count, 2 * leaves, share), jnp.float32),
            pltpu.VMEM((n_sub, count, leaves, share), jnp.float32),
            pltpu.VMEM((n_sub, count, leaves, share), jnp.float32),
            pltpu.VMEM((n_sub, leaves, share), jnp.float32),
            pltpu.VMEM((n_sub, leaves, share), jnp.float32),
            pltpu.VMEM((n_leaf * n_sub, 1, LANES), jnp.float32),
            pltpu.SemaphoreType.DMA((4 * n_sub + 1,)),
            pltpu.SemaphoreType.DMA((4 * n_sub + 1,)),
        ],
        compiler_params=pltpu.CompilerParams(
            collective_id=collective_id, has_side_effects=True, vmem_limit_bytes=VMEM_LIMIT
        ),
    )(*args)


def block_lists(offsets, counts):
    leaves, slots = offsets.shape
    total_leaves = leaves * lax.axis_size("leaf")
    anchor = jnp.arange(leaves, dtype=jnp.int32)[:, None]
    target = anchor + offsets
    slot_idx = jnp.arange(slots, dtype=jnp.int32)[None, :]
    usable = (slot_idx < counts[:, None]) & (target + lax.axis_index("leaf") * leaves < total_leaves)
    used = jnp.concatenate([jnp.ones((leaves, 1), bool), usable], axis=1).reshape(-1)
    cols = jnp.concatenate([anchor, target], axis=1).reshape(-1)
    rows = jnp.broadcast_to(anchor, (leaves, slots + 1)).reshape(-1)
    mirrors = jnp.concatenate([jnp.full((leaves, 1), 2 * leaves, jnp.int32), target], axis=1).reshape(-1)
    size = rows.shape[0]
    idx = jnp.arange(size, dtype=jnp.int32)
    used_i = used.astype(jnp.int32)
    before = jnp.sum(jnp.where(idx[None, :] < idx[:, None], used_i[None, :], 0), axis=1)
    length = -(-size // GROUP) * GROUP
    place = jnp.arange(length, dtype=jnp.int32)
    hit = (before[None, :] == place[:, None]) & used[None, :]
    any_hit = jnp.sum(hit.astype(jnp.int32), axis=1)

    def compact(values, fill):
        return jnp.sum(jnp.where(hit, values[None, :], 0), axis=1) + (1 - any_hit) * fill

    count = jnp.sum(used_i)
    return (
        compact(rows, leaves),
        compact(cols, 0),
        compact(mirrors, 2 * leaves),
        ((count + GROUP - 1) // GROUP).reshape((1,)),
    )


def body(features, occupancy, offsets, counts, right_side):
    leaves, share = right_side.shape
    n_sub = lax.axis_size("sub")
    voxels = share * n_sub
    feat = features.shape[1] * n_sub // voxels
    occ = occupancy.astype(jnp.float32)
    masked = occ * right_side
    part = feat // n_sub
    slab = features.reshape((leaves, part, voxels)).reshape((leaves * part, voxels))
    own_slabs, ahead_slabs, window = gather_all(slab, masked)
    lists = block_lists(offsets, counts)
    col_feat = jnp.concatenate([own_slabs, ahead_slabs]).reshape((2, n_sub, leaves, part, voxels))
    col_feat = col_feat.transpose((0, 2, 1, 3, 4)).reshape((2 * leaves, feat, voxels))
    scale = 1.0 / (2.0 * feat)
    col_w = jnp.exp(-scale * jnp.sum(jnp.square(col_feat.astype(jnp.float32)), axis=1))
    start = lax.axis_index("sub") * share
    own_rows = lax.dynamic_slice_in_dim(col_feat[:leaves], start, share, 2)
    row_w = lax.dynamic_slice_in_dim(col_w[:leaves], start, share, 1)
    row_feat = own_rows.transpose((0, 2, 1)) * jnp.bfloat16(2.0 * scale)
    feats = (row_feat, col_feat, row_w, col_w)

    fwd, mir = apply_blocks(True, lists, feats, masked, window)
    x, res, direction, u, win_dir, win_res, diagonal = update(
        True, False, 0, (fwd, mir, occ, right_side, window)
    )
    for it in range(1, ITERS):
        fwd, mir = apply_blocks(False, lists, feats, u, win_dir)
        args = (fwd, mir, occ, direction, diagonal, x, res)
        if it == ITERS - 1:
            x, res = update(False, True, it, args)
        else:
            x, res, direction, u, win_dir, win_res = update(
                False, False, it, args + (win_dir, win_res)
            )
    return x, res


def solution(mesh):
    in_specs = (
        P(("groups", "leaf"), "sub"),
        P(("groups", "leaf"), "sub"),
        P(("groups", "leaf"), None),
        P(("groups", "leaf")),
        P(("groups", "leaf"), "sub"),
    )
    out_specs = (P(("groups", "leaf"), "sub"), P(("groups", "leaf"), "sub"))
    return jax.shard_map(body, mesh=mesh, in_specs=in_specs, out_specs=out_specs, check_vma=False)
```

```python
import functools

import jax
import jax.numpy as jnp
from jax import lax
from jax.experimental import pallas as pl
from jax.experimental.pallas import tpu as pltpu
from jax.sharding import PartitionSpec as P

ITERS = 3
GROUP = 32
LANES = 128
VMEM_LIMIT = 48 * 1024 * 1024
diag_shift = 0.25
MESH = pl.DeviceIdType.MESH


def pack(x):
    k = max(1, LANES // x.shape[1])
    rows = x.shape[0] // k
    return jnp.concatenate([x[i * rows:(i + 1) * rows] for i in range(k)], axis=1)


def unpack(x, share):
    return jnp.concatenate([x[:, i:i + share] for i in range(0, x.shape[1], share)], axis=0)


def packed_shape(leaves, share):
    k = max(1, LANES // share)
    return (leaves // k, share * k)


def apply_kernel(with_ones, rows_at, cols_at, mirror_at, groups_ref, row_ref, col_ref, row_w_ref, col_w_ref, u_ref, v_ref,
                 fwd_ref, mir_ref, u_wide, v_scaled, fwd_acc, mir_acc):
    leaves, share = u_ref.shape
    voxels = v_ref.shape[1]
    count = fwd_ref.shape[0]
    row_w = row_w_ref[...]
    col_w = col_w_ref[...]
    u_wide[0] = jnp.broadcast_to((u_ref[...] * row_w)[:, :, None], u_wide.shape[1:])
    v_scaled[0] = v_ref[...] * col_w
    if with_ones:
        u_wide[1] = jnp.broadcast_to(row_w[:, :, None], u_wide.shape[1:])
        v_scaled[1] = col_w
    fwd_acc[...] = jnp.zeros_like(fwd_acc)
    mir_acc[...] = jnp.zeros_like(mir_acc)

    def fold_lanes(x):
        return sum(x[:, i:i + LANES] for i in range(0, voxels, LANES))

    def fold_rows(x):
        return sum(x[i:i + 8, :] for i in range(0, share, 8))

    def group(g, carry):
        marks, blocks = [], []
        for i in range(GROUP):
            at = g * GROUP + i
            marks.append((rows_at[at], cols_at[at], mirror_at[at]))
        for row, col, mir in marks:
            blocks.append(jnp.exp(jnp.dot(
                row_ref[jnp.minimum(row, leaves - 1)], col_ref[col],
                preferred_element_type=jnp.float32,
            )))
        for (row, col, mir), block in zip(marks, blocks):
            row_read = jnp.minimum(row, leaves - 1)
            for n in range(count):
                wide = jnp.concatenate([u_wide[n, row_read]] * (voxels // LANES), axis=1)
                fwd_acc[n, row] += fold_lanes(block * v_scaled[n, pl.ds(col, 1), :])
                mir_acc[n, mir] += fold_rows(block * wide)
        return carry

    lax.fori_loop(0, groups_ref[0], group, 0)
    for n in range(count):
        fwd_ref[n] = jnp.sum(fwd_acc[n, :leaves], axis=-1) * row_w
        mir_ref[n] = jnp.sum(mir_acc[n, :2 * leaves], axis=1) * col_w


def apply_blocks(with_ones, lists, feats, u, v):
    leaves, share = u.shape
    voxels = v.shape[1]
    count = 2 if with_ones else 1
    smem = pl.BlockSpec(memory_space=pltpu.SMEM)
    vmem = pl.BlockSpec(memory_space=pltpu.VMEM)
    return pl.pallas_call(
        functools.partial(apply_kernel, with_ones),
        out_shape=(
            jax.ShapeDtypeStruct((count, leaves, share), jnp.float32),
            jax.ShapeDtypeStruct((count, 2 * leaves, voxels), jnp.float32),
        ),
        in_specs=[smem] * 4 + [vmem] * 6,
        out_specs=(vmem, vmem),
        scratch_shapes=[
            pltpu.VMEM((count, leaves, share, LANES), jnp.float32),
            pltpu.VMEM((count, 2 * leaves, voxels), jnp.float32),
            pltpu.VMEM((count, leaves + 1, share, LANES), jnp.float32),
            pltpu.VMEM((count, 2 * leaves + 1, 8, voxels), jnp.float32),
        ],
        compiler_params=pltpu.CompilerParams(vmem_limit_bytes=VMEM_LIMIT),
    )(*lists, *feats, u, v)


def gather_kernel(n_leaf, n_sub, slab_ref, field_ref, own_out, ahead_out, window_out,
                  field_own, field_ahead, send_sem, recv_sem, field_send, field_recv):
    group_at = lax.axis_index("groups")
    leaf_at = lax.axis_index("leaf")
    sub_at = lax.axis_index("sub")
    inner = 2 if n_sub % 2 == 0 else 1
    n_out = n_sub // inner
    out_at = sub_at // inner
    in_at = sub_at % inner
    leaves, share = field_ref.shape
    behind = lax.rem(leaf_at + n_leaf - 1, n_leaf)
    devices = n_leaf * n_sub

    barrier = pltpu.get_barrier_semaphore()

    def greet(k, carry):
        to = (
            group_at,
            lax.rem(leaf_at + k // n_sub, n_leaf),
            lax.rem(sub_at + k % n_sub, n_sub),
        )
        pl.semaphore_signal(barrier, inc=1, device_id=to, device_id_type=MESH)
        return carry

    lax.fori_loop(1, devices, greet, 0)
    field_own[0] = pack(field_ref[...])
    pl.semaphore_wait(barrier, devices - 1)

    sent = []

    def send(src, dst, slot, leaf, sub):
        c = pltpu.make_async_remote_copy(
            src_ref=src, dst_ref=dst, send_sem=send_sem.at[len(sent)], recv_sem=recv_sem.at[slot],
            device_id=(group_at, leaf, sub), device_id_type=MESH,
        )
        c.start()
        sent.append(c)

    def arrived(dst, slot):
        pltpu.make_async_remote_copy(
            src_ref=slab_ref, dst_ref=dst, send_sem=send_sem.at[0], recv_sem=recv_sem.at[slot],
            device_id=(group_at, leaf_at, sub_at), device_id_type=MESH,
        ).wait_recv()

    def sub_of(outer_by, other):
        return lax.rem(out_at + outer_by, n_out) * inner + (inner - 1 - in_at if other else in_at)

    partner = sub_of(0, True)
    send(slab_ref, ahead_out.at[sub_at], n_sub + sub_at, behind, sub_at)
    for d in range(1, n_out):
        send(slab_ref, own_out.at[sub_at], sub_at, leaf_at, sub_of(d, False))
    if inner == 2:
        send(slab_ref, own_out.at[sub_at], sub_at, leaf_at, partner)
    field_copies = []
    for s in range(n_sub):
        to = lax.rem(sub_at + s, n_sub)
        field_copies.append(pltpu.make_async_remote_copy(
            src_ref=field_own.at[0], dst_ref=field_ahead.at[s],
            send_sem=field_send.at[s], recv_sem=field_recv.at[s],
            device_id=(group_at, behind, to), device_id_type=MESH,
        ))
        if s:
            field_copies.append(pltpu.make_async_remote_copy(
                src_ref=field_own.at[0], dst_ref=field_own.at[s],
                send_sem=field_send.at[n_sub + s], recv_sem=field_recv.at[n_sub + s],
                device_id=(group_at, leaf_at, to), device_id_type=MESH,
            ))
    for c in field_copies:
        c.start()
    own_out[sub_at] = slab_ref[...]
    arrived(ahead_out.at[sub_at], n_sub + sub_at)
    for d in range(1, n_out):
        send(ahead_out.at[sub_at], ahead_out.at[sub_at], n_sub + sub_at, leaf_at, sub_of(d, False))
    if inner == 2:
        send(ahead_out.at[sub_at], ahead_out.at[sub_at], n_sub + sub_at, leaf_at, partner)
    for base, out in ((0, own_out), (n_sub, ahead_out)):
        for d in range(1, n_out):
            slot = sub_of(n_out - d, False)
            arrived(out.at[slot], base + slot)
            if inner == 2:
                send(out.at[slot], out.at[slot], base + slot, leaf_at, partner)
    for c in field_copies:
        c.wait()
    for part, held in enumerate((field_own, field_ahead)):
        window_out[part * leaves:(part + 1) * leaves, :] = jnp.concatenate(
            [unpack(held[lax.rem(sub_at - s + n_sub, n_sub)], share) for s in range(n_sub)], axis=1
        )
    if inner == 2:
        for base, out in ((0, own_out), (n_sub, ahead_out)):
            for d in range(n_out):
                slot = sub_of(n_out - d, True)
                arrived(out.at[slot], base + slot)
    for c in sent:
        c.wait_send()


def gather_all(slab, field):
    n_leaf, n_sub = lax.axis_size("leaf"), lax.axis_size("sub")
    leaves, share = field.shape
    vmem = pl.BlockSpec(memory_space=pltpu.VMEM)
    slabs = jax.ShapeDtypeStruct((n_sub,) + slab.shape, slab.dtype)
    return pl.pallas_call(
        functools.partial(gather_kernel, n_leaf, n_sub),
        out_shape=(slabs, slabs, jax.ShapeDtypeStruct((2 * leaves, share * n_sub), jnp.float32)),
        in_specs=[vmem] * 2,
        out_specs=(vmem,) * 3,
        scratch_shapes=[
            pltpu.VMEM((n_sub,) + packed_shape(leaves, share), jnp.float32),
            pltpu.VMEM((n_sub,) + packed_shape(leaves, share), jnp.float32),
            pltpu.SemaphoreType.DMA((3 * n_sub + 2,)),
            pltpu.SemaphoreType.DMA((2 * n_sub,)),
            pltpu.SemaphoreType.DMA((2 * n_sub,)),
            pltpu.SemaphoreType.DMA((2 * n_sub,)),
        ],
        compiler_params=pltpu.CompilerParams(
            collective_id=ITERS, has_side_effects=True, vmem_limit_bytes=VMEM_LIMIT
        ),
    )(slab, field)


def update_kernel(first, last, n_leaf, n_sub, *refs):
    refs = list(refs)
    fwd_ref, mir_ref, occ_ref, dir_ref = refs[:4]
    del refs[:4]
    if first:
        window_ref = refs.pop(0)
        out_refs = refs[:8]
        del refs[:8]
        x_out, res_out, dir_out, u_out, win_dir_out, win_res_out, diag_out, occ_out = out_refs
    else:
        diag_ref, x_ref, res_ref = refs[:3]
        del refs[:3]
        if last:
            x_out, res_out = refs[:2]
            del refs[:2]
        else:
            win_dir_ref, win_res_ref = refs[:2]
            x_out, res_out, dir_out, u_out, win_dir_out, win_res_out = refs[2:8]
            del refs[:8]
    mir_send, mir_own, mir_back, img_own, img_ahead, scalars, send_sem, recv_sem = refs

    group_at = lax.axis_index("groups")
    leaf_at = lax.axis_index("leaf")
    sub_at = lax.axis_index("sub")
    devices = n_leaf * n_sub
    leaves, share = fwd_ref.shape[1:]
    voxels = share * n_sub
    count = fwd_ref.shape[0]

    def peer(leaf_by, sub_by):
        return (
            group_at,
            lax.rem(leaf_at + leaf_by, n_leaf),
            lax.rem(sub_at + sub_by, n_sub),
        )

    barrier = pltpu.get_barrier_semaphore()

    def greet(k, carry):
        pl.semaphore_signal(barrier, inc=1, device_id=peer(k // n_sub, k % n_sub), device_id_type=MESH)
        return carry

    lax.fori_loop(1, devices, greet, 0)
    for s in range(n_sub):
        for n in range(count):
            for part in range(2):
                mir_send[s, part, n] = pack(
                    mir_ref[n, part * leaves:(part + 1) * leaves, s * share:(s + 1) * share]
                )
    pl.semaphore_wait(barrier, devices - 1)

    def copy(src, dst, sem, leaf_by, sub_by):
        return pltpu.make_async_remote_copy(
            src_ref=src, dst_ref=dst, send_sem=send_sem.at[sem], recv_sem=recv_sem.at[sem],
            device_id=peer(leaf_by, sub_by), device_id_type=MESH,
        )

    copies = []
    for s in range(n_sub):
        to = lax.rem(sub_at + s, n_sub)
        copies.append(copy(mir_send.at[to, 1], mir_back.at[s], s, 1, s))
        copies[-1].start()
    for s in range(1, n_sub):
        to = lax.rem(sub_at + s, n_sub)
        copies.append(copy(mir_send.at[to, 0], mir_own.at[s], n_sub + s, 0, s))
        copies[-1].start()
    total = [pack(fwd_ref[n]) + mir_send[sub_at, 0, n] for n in range(count)]
    for c in copies:
        c.wait()
    for n in range(count):
        for s in range(1, n_sub):
            total[n] += mir_own[s, n]
        for s in range(n_sub):
            total[n] += mir_back[s, n]
    occ = occ_ref[...]
    direction = dir_ref[...]
    if first:
        occ = pack(occ)
        direction = pack(direction)
        occ_out[...] = occ
    if first:
        diagonal = diag_shift + total[1] / voxels
        residual = direction
        field = jnp.zeros_like(direction)
        diag_out[...] = diagonal
    else:
        diagonal = diag_ref[...]
        residual = res_ref[...]
        field = x_ref[...]
    image = diagonal * direction + occ * total[0] / voxels
    sums = (residual * residual, direction * image, residual * image, image * image)
    for i, term in enumerate(sums):
        scalars[0, i:i + 1, :] = jnp.sum(term, axis=0, keepdims=True)

    def tell(k, carry):
        copy(scalars.at[0], scalars.at[k], 4 * n_sub, k // n_sub, k % n_sub).start()
        return carry

    lax.fori_loop(1, devices, tell, 0)
    copies = []
    if not last:
        img_own[0] = occ * image
        for s in range(n_sub):
            copies.append(copy(img_own.at[0], img_ahead.at[s], 2 * n_sub + s, n_leaf - 1, s))
            copies[-1].start()
        for s in range(1, n_sub):
            copies.append(copy(img_own.at[0], img_own.at[s], 3 * n_sub + s, 0, s))
            copies[-1].start()
    everyone = copy(scalars.at[1:], scalars.at[1:], 4 * n_sub, 1, 0)
    everyone.wait()
    sums = jnp.sum(scalars[...], axis=0)
    sums = jnp.sum(sums, axis=1, keepdims=True)
    rr, dq, rq, qq = [sums[i:i + 1] for i in range(4)]
    step = rr / dq
    new = rr - 2.0 * step * rq + step * step * qq
    beta = new / rr
    field = field + step * direction
    residual = residual - step * image
    if last:
        x_out[...] = unpack(field, share)
        res_out[...] = unpack(residual, share)
        return
    x_out[...] = field
    res_out[...] = residual
    direction = residual + beta * direction
    dir_out[...] = direction
    u_out[...] = unpack(occ * direction, share)
    for c in copies:
        c.wait()
    if first:
        win_dir_ref = win_res_ref = window_ref
    for part, held in enumerate((img_own, img_ahead)):
        image_window = jnp.concatenate(
            [unpack(held[lax.rem(sub_at - s + n_sub, n_sub)], share) for s in range(n_sub)], axis=1
        )
        rows = slice(part * leaves, (part + 1) * leaves)
        res_window = win_res_ref[rows, :] - step * image_window
        win_res_out[rows, :] = res_window
        win_dir_out[rows, :] = res_window + beta * win_dir_ref[rows, :]


def update(first, last, collective_id, args):
    n_leaf, n_sub = lax.axis_size("leaf"), lax.axis_size("sub")
    count = 2 if first else 1
    leaves, share = args[0].shape[1:]
    voxels = share * n_sub
    shape = packed_shape(leaves, share)
    packed = jax.ShapeDtypeStruct(shape, jnp.float32)
    own = jax.ShapeDtypeStruct((leaves, share), jnp.float32)
    window = jax.ShapeDtypeStruct((2 * leaves, voxels), jnp.float32)
    out_shape = (own, own) if last else (packed, packed, packed, own, window, window)
    if first:
        out_shape = out_shape + (packed, packed)
    vmem = pl.BlockSpec(memory_space=pltpu.VMEM)
    return pl.pallas_call(
        functools.partial(update_kernel, first, last, n_leaf, n_sub),
        out_shape=out_shape,
        in_specs=[vmem] * len(args),
        out_specs=(vmem,) * len(out_shape),
        scratch_shapes=[
            pltpu.VMEM((n_sub, 2, count) + shape, jnp.float32),
            pltpu.VMEM((n_sub, count) + shape, jnp.float32),
            pltpu.VMEM((n_sub, count) + shape, jnp.float32),
            pltpu.VMEM((n_sub,) + shape, jnp.float32),
            pltpu.VMEM((n_sub,) + shape, jnp.float32),
            pltpu.VMEM((n_leaf * n_sub, 4, shape[1]), jnp.float32),
            pltpu.SemaphoreType.DMA((4 * n_sub + 1,)),
            pltpu.SemaphoreType.DMA((4 * n_sub + 1,)),
        ],
        compiler_params=pltpu.CompilerParams(
            collective_id=collective_id, has_side_effects=True, vmem_limit_bytes=VMEM_LIMIT
        ),
    )(*args)


def block_lists(offsets, counts):
    leaves, slots = offsets.shape
    total_leaves = leaves * lax.axis_size("leaf")
    anchor = jnp.arange(leaves, dtype=jnp.int32)[:, None]
    target = anchor + offsets
    slot_idx = jnp.arange(slots, dtype=jnp.int32)[None, :]
    usable = (slot_idx < counts[:, None]) & (target + lax.axis_index("leaf") * leaves < total_leaves)
    used = jnp.concatenate([jnp.ones((leaves, 1), bool), usable], axis=1).reshape(-1)
    cols = jnp.concatenate([anchor, target], axis=1).reshape(-1)
    rows = jnp.broadcast_to(anchor, (leaves, slots + 1)).reshape(-1)
    mirrors = jnp.concatenate([jnp.full((leaves, 1), 2 * leaves, jnp.int32), target], axis=1).reshape(-1)
    size = rows.shape[0]
    idx = jnp.arange(size, dtype=jnp.int32)
    used_i = used.astype(jnp.int32)
    before = jnp.sum(jnp.where(idx[None, :] < idx[:, None], used_i[None, :], 0), axis=1)
    length = -(-size // GROUP) * GROUP
    place = jnp.arange(length, dtype=jnp.int32)
    hit = (before[None, :] == place[:, None]) & used[None, :]
    any_hit = jnp.sum(hit.astype(jnp.int32), axis=1)

    def compact(values, fill):
        return jnp.sum(jnp.where(hit, values[None, :], 0), axis=1) + (1 - any_hit) * fill

    count = jnp.sum(used_i)
    return (
        compact(rows, leaves),
        compact(cols, 0),
        compact(mirrors, 2 * leaves),
        ((count + GROUP - 1) // GROUP).reshape((1,)),
    )


def body(features, occupancy, offsets, counts, right_side):
    leaves, share = right_side.shape
    n_sub = lax.axis_size("sub")
    voxels = share * n_sub
    feat = features.shape[1] * n_sub // voxels
    occ = occupancy.astype(jnp.float32)
    masked = occ * right_side
    part = feat // n_sub
    slab = features.reshape((leaves, part, voxels)).reshape((leaves * part, voxels))
    own_slabs, ahead_slabs, window = gather_all(slab, masked)
    lists = block_lists(offsets, counts)
    col_feat = jnp.concatenate([own_slabs, ahead_slabs]).reshape((2, n_sub, leaves, part, voxels))
    col_feat = col_feat.transpose((0, 2, 1, 3, 4)).reshape((2 * leaves, feat, voxels))
    scale = 1.0 / (2.0 * feat)
    col_w = jnp.exp(-scale * jnp.sum(jnp.square(col_feat.astype(jnp.float32)), axis=1))
    start = lax.axis_index("sub") * share
    own_rows = lax.dynamic_slice_in_dim(col_feat[:leaves], start, share, 2)
    row_w = lax.dynamic_slice_in_dim(col_w[:leaves], start, share, 1)
    row_feat = own_rows.transpose((0, 2, 1)) * jnp.bfloat16(2.0 * scale)
    feats = (row_feat, col_feat, row_w, col_w)

    fwd, mir = apply_blocks(True, lists, feats, masked, window)
    x, res, direction, u, win_dir, win_res, diagonal, occ = update(
        True, False, 0, (fwd, mir, occ, right_side, window)
    )
    for it in range(1, ITERS):
        fwd, mir = apply_blocks(False, lists, feats, u, win_dir)
        args = (fwd, mir, occ, direction, diagonal, x, res)
        if it == ITERS - 1:
            x, res = update(False, True, it, args)
        else:
            x, res, direction, u, win_dir, win_res = update(
                False, False, it, args + (win_dir, win_res)
            )
    return x, res


def solution(mesh):
    in_specs = (
        P(("groups", "leaf"), "sub"),
        P(("groups", "leaf"), "sub"),
        P(("groups", "leaf"), None),
        P(("groups", "leaf")),
        P(("groups", "leaf"), "sub"),
    )
    out_specs = (P(("groups", "leaf"), "sub"), P(("groups", "leaf"), "sub"))
    return jax.shard_map(body, mesh=mesh, in_specs=in_specs, out_specs=out_specs, check_vma=False)
```

```python
import functools

import jax
import jax.numpy as jnp
from jax import lax
from jax.experimental import pallas as pl
from jax.experimental.pallas import tpu as pltpu
from jax.sharding import PartitionSpec as P

ITERS = 3
GROUP = 32
LANES = 128
VMEM_LIMIT = 48 * 1024 * 1024
diag_shift = 0.25
MESH = pl.DeviceIdType.MESH


def pack(x):
    k = max(1, LANES // x.shape[1])
    rows = x.shape[0] // k
    return jnp.concatenate([x[i * rows:(i + 1) * rows] for i in range(k)], axis=1)


def unpack(x, share):
    return jnp.concatenate([x[:, i:i + share] for i in range(0, x.shape[1], share)], axis=0)


def packed_shape(leaves, share):
    k = max(1, LANES // share)
    return (leaves // k, share * k)


def apply_kernel(with_ones, codes_ref, row_ref, col_ref, row_w_ref, col_w_ref, u_ref, v_ref,
                 fwd_ref, mir_ref, u_wide, v_scaled, fwd_acc, mir_acc):
    leaves, share = u_ref.shape
    voxels = v_ref.shape[1]
    count = fwd_ref.shape[0]
    row_w = row_w_ref[...]
    col_w = col_w_ref[...]
    u_wide[0] = jnp.broadcast_to((u_ref[...] * row_w)[:, :, None], u_wide.shape[1:])
    v_scaled[0] = v_ref[...] * col_w
    if with_ones:
        u_wide[1] = jnp.broadcast_to(row_w[:, :, None], u_wide.shape[1:])
        v_scaled[1] = col_w
    fwd_acc[...] = jnp.zeros_like(fwd_acc)
    mir_acc[...] = jnp.zeros_like(mir_acc)

    def fold_lanes(x):
        return sum(x[:, i:i + LANES] for i in range(0, voxels, LANES))

    def fold_rows(x):
        return sum(x[i:i + 8, :] for i in range(0, share, 8))

    def group(g, carry):
        marks, blocks = [], []
        for i in range(GROUP):
            at = g * GROUP + i
            code = codes_ref[0, at]
            row = code // (4 * leaves)
            col = code % (4 * leaves)
            marks.append((row, col, jnp.where(row == col, 2 * leaves, col)))
        for row, col, mir in marks:
            blocks.append(jnp.exp(jnp.dot(
                row_ref[jnp.minimum(row, leaves - 1)], col_ref[col],
                preferred_element_type=jnp.float32,
            )))
        for (row, col, mir), block in zip(marks, blocks):
            row_read = jnp.minimum(row, leaves - 1)
            for n in range(count):
                wide = jnp.concatenate([u_wide[n, row_read]] * (voxels // LANES), axis=1)
                fwd_acc[n, row] += fold_lanes(block * v_scaled[n, pl.ds(col, 1), :])
                mir_acc[n, mir] += fold_rows(block * wide)
        return carry

    lax.fori_loop(0, codes_ref[0, codes_ref.shape[1] - 1], group, 0)
    for n in range(count):
        fwd_ref[n] = jnp.sum(fwd_acc[n, :leaves], axis=-1) * row_w
        mir_ref[n] = jnp.sum(mir_acc[n, :2 * leaves], axis=1) * col_w


def apply_blocks(with_ones, codes, feats, u, v):
    leaves, share = u.shape
    voxels = v.shape[1]
    count = 2 if with_ones else 1
    smem = pl.BlockSpec(memory_space=pltpu.SMEM)
    vmem = pl.BlockSpec(memory_space=pltpu.VMEM)
    return pl.pallas_call(
        functools.partial(apply_kernel, with_ones),
        out_shape=(
            jax.ShapeDtypeStruct((count, leaves, share), jnp.float32),
            jax.ShapeDtypeStruct((count, 2 * leaves, voxels), jnp.float32),
        ),
        in_specs=[smem] + [vmem] * 6,
        out_specs=(vmem, vmem),
        scratch_shapes=[
            pltpu.VMEM((count, leaves, share, LANES), jnp.float32),
            pltpu.VMEM((count, 2 * leaves, voxels), jnp.float32),
            pltpu.VMEM((count, leaves + 1, share, LANES), jnp.float32),
            pltpu.VMEM((count, 2 * leaves + 1, 8, voxels), jnp.float32),
        ],
        compiler_params=pltpu.CompilerParams(vmem_limit_bytes=VMEM_LIMIT),
    )(codes, *feats, u, v)


def used_blocks(offsets, counts, leaf_at, total_leaves, width):
    leaves, slots = offsets.shape
    row = lax.broadcasted_iota(jnp.int32, (leaves, 1), 0)
    place = lax.broadcasted_iota(jnp.int32, (leaves, width), 1)
    targets, used = [row], [jnp.ones((leaves, 1), jnp.int32)]
    for j in range(slots):
        target = row + offsets[:, j:j + 1]
        fits = (counts > j) & (target + leaf_at * leaves < total_leaves)
        targets.append(target)
        used.append(fits.astype(jnp.int32))
    row_count = sum(used).astype(jnp.float32)
    earlier = (
        lax.broadcasted_iota(jnp.int32, (leaves, leaves), 1)
        < lax.broadcasted_iota(jnp.int32, (leaves, leaves), 0)
    ).astype(jnp.float32)
    at = jnp.dot(
        earlier, jnp.broadcast_to(row_count, (leaves, LANES)), preferred_element_type=jnp.float32
    )[:, :1].astype(jnp.int32)
    filler = leaves * 4 * leaves + leaves
    codes = jnp.zeros((leaves, width), jnp.int32)
    for target, use in zip(targets, used):
        hit = (place == at) & (use > 0)
        codes = codes + jnp.where(hit, row * (4 * leaves) + target - filler, 0)
        at = at + use
    codes = jnp.sum(codes, axis=0, keepdims=True) + filler
    turns = (jnp.sum(row_count, axis=0, keepdims=True).astype(jnp.int32) + (GROUP - 1)) // GROUP
    return jnp.where(place[:1] == width - 1, turns, codes)


def gather_kernel(n_leaf, n_sub, slab_ref, field_ref, offsets_ref, counts_ref,
                  own_out, ahead_out, window_out, codes_out,
                  field_own, field_ahead, send_sem, recv_sem, field_send, field_recv):
    group_at = lax.axis_index("groups")
    leaf_at = lax.axis_index("leaf")
    sub_at = lax.axis_index("sub")
    inner = 2 if n_sub % 2 == 0 else 1
    n_out = n_sub // inner
    out_at = sub_at // inner
    in_at = sub_at % inner
    leaves, share = field_ref.shape
    behind = lax.rem(leaf_at + n_leaf - 1, n_leaf)
    devices = n_leaf * n_sub

    barrier = pltpu.get_barrier_semaphore()

    def greet(k, carry):
        to = (
            group_at,
            lax.rem(leaf_at + k // n_sub, n_leaf),
            lax.rem(sub_at + k % n_sub, n_sub),
        )
        pl.semaphore_signal(barrier, inc=1, device_id=to, device_id_type=MESH)
        return carry

    lax.fori_loop(1, devices, greet, 0)
    field_own[0] = pack(field_ref[...])
    pl.semaphore_wait(barrier, devices - 1)

    sent = []

    def send(src, dst, slot, leaf, sub):
        c = pltpu.make_async_remote_copy(
            src_ref=src, dst_ref=dst, send_sem=send_sem.at[len(sent)], recv_sem=recv_sem.at[slot],
            device_id=(group_at, leaf, sub), device_id_type=MESH,
        )
        c.start()
        sent.append(c)

    half = slab_ref.shape[0] // 2

    def arrived(dst, slot, src=slab_ref):
        pltpu.make_async_remote_copy(
            src_ref=src, dst_ref=dst, send_sem=send_sem.at[0], recv_sem=recv_sem.at[slot],
            device_id=(group_at, leaf_at, sub_at), device_id_type=MESH,
        ).wait_recv()

    def sub_of(outer_by, other):
        return lax.rem(out_at + outer_by, n_out) * inner + (inner - 1 - in_at if other else in_at)

    partner = sub_of(0, True)
    send(slab_ref, ahead_out.at[sub_at], n_sub + sub_at, behind, sub_at)
    for d in range(1, n_out):
        send(slab_ref, own_out.at[sub_at], sub_at, leaf_at, sub_of(d, False))
    if inner == 2:
        send(slab_ref, own_out.at[sub_at], sub_at, leaf_at, partner)
    field_copies = []
    for s in range(n_sub):
        to = lax.rem(sub_at + s, n_sub)
        field_copies.append(pltpu.make_async_remote_copy(
            src_ref=field_own.at[0], dst_ref=field_ahead.at[s],
            send_sem=field_send.at[s], recv_sem=field_recv.at[s],
            device_id=(group_at, behind, to), device_id_type=MESH,
        ))
        if s:
            field_copies.append(pltpu.make_async_remote_copy(
                src_ref=field_own.at[0], dst_ref=field_own.at[s],
                send_sem=field_send.at[n_sub + s], recv_sem=field_recv.at[n_sub + s],
                device_id=(group_at, leaf_at, to), device_id_type=MESH,
            ))
    for c in field_copies:
        c.start()
    own_out[sub_at] = slab_ref[...]
    codes_out[...] = used_blocks(
        offsets_ref[...], counts_ref[...], leaf_at, n_leaf * leaves, codes_out.shape[1]
    )
    arrived(ahead_out.at[sub_at], n_sub + sub_at)
    low, high = pl.ds(0, half), pl.ds(half, half)
    for d in range(1, n_out):
        send(ahead_out.at[sub_at, low], ahead_out.at[sub_at, low], n_sub + sub_at, leaf_at, sub_of(d, False))
    for d in range(1, n_out):
        slot = sub_of(n_out - d, False)
        arrived(own_out.at[slot], slot)
        send(own_out.at[slot, high], ahead_out.at[slot, high], 2 * n_sub + slot, behind, sub_at)
        if inner == 2:
            send(own_out.at[slot], own_out.at[slot], slot, leaf_at, partner)
    if inner == 2:
        send(ahead_out.at[sub_at], ahead_out.at[sub_at], n_sub + sub_at, leaf_at, partner)
    for d in range(1, n_out):
        slot = sub_of(n_out - d, False)
        arrived(ahead_out.at[slot, low], n_sub + slot, slab_ref.at[low])
        arrived(ahead_out.at[slot, high], 2 * n_sub + slot, slab_ref.at[high])
        if inner == 2:
            send(ahead_out.at[slot], ahead_out.at[slot], n_sub + slot, leaf_at, partner)
    for c in field_copies:
        c.wait()
    for part, held in enumerate((field_own, field_ahead)):
        window_out[part * leaves:(part + 1) * leaves, :] = jnp.concatenate(
            [unpack(held[lax.rem(sub_at - s + n_sub, n_sub)], share) for s in range(n_sub)], axis=1
        )
    if inner == 2:
        for base, out in ((0, own_out), (n_sub, ahead_out)):
            for d in range(n_out):
                slot = sub_of(n_out - d, True)
                arrived(out.at[slot], base + slot)
    for c in sent:
        c.wait_send()


def gather_all(slab, field, offsets, counts):
    n_leaf, n_sub = lax.axis_size("leaf"), lax.axis_size("sub")
    leaves, share = field.shape
    vmem = pl.BlockSpec(memory_space=pltpu.VMEM)
    slabs = jax.ShapeDtypeStruct((n_sub,) + slab.shape, slab.dtype)
    length = -(-leaves * (offsets.shape[1] + 1) // LANES) * LANES
    return pl.pallas_call(
        functools.partial(gather_kernel, n_leaf, n_sub),
        out_shape=(slabs, slabs, jax.ShapeDtypeStruct((2 * leaves, share * n_sub), jnp.float32),
                   jax.ShapeDtypeStruct((1, length + LANES), jnp.int32)),
        in_specs=[vmem] * 4,
        out_specs=(vmem,) * 4,
        scratch_shapes=[
            pltpu.VMEM((n_sub,) + packed_shape(leaves, share), jnp.float32),
            pltpu.VMEM((n_sub,) + packed_shape(leaves, share), jnp.float32),
            pltpu.SemaphoreType.DMA((3 * n_sub + 2,)),
            pltpu.SemaphoreType.DMA((3 * n_sub,)),
            pltpu.SemaphoreType.DMA((2 * n_sub,)),
            pltpu.SemaphoreType.DMA((2 * n_sub,)),
        ],
        compiler_params=pltpu.CompilerParams(
            collective_id=ITERS, has_side_effects=True, vmem_limit_bytes=VMEM_LIMIT
        ),
    )(slab, field, offsets, counts[:, None])


def update_kernel(first, last, n_leaf, n_sub, *refs):
    refs = list(refs)
    fwd_ref, mir_ref, occ_ref, dir_ref = refs[:4]
    del refs[:4]
    if first:
        window_ref = refs.pop(0)
        out_refs = refs[:8]
        del refs[:8]
        x_out, res_out, dir_out, u_out, win_dir_out, win_res_out, diag_out, occ_out = out_refs
    else:
        diag_ref, x_ref, res_ref = refs[:3]
        del refs[:3]
        if last:
            x_out, res_out = refs[:2]
            del refs[:2]
        else:
            win_dir_ref, win_res_ref = refs[:2]
            x_out, res_out, dir_out, u_out, win_dir_out, win_res_out = refs[2:8]
            del refs[:8]
    mir_send, mir_own, mir_back, img_own, img_ahead, scalars, send_sem, recv_sem = refs

    group_at = lax.axis_index("groups")
    leaf_at = lax.axis_index("leaf")
    sub_at = lax.axis_index("sub")
    devices = n_leaf * n_sub
    leaves, share = fwd_ref.shape[1:]
    voxels = share * n_sub
    count = fwd_ref.shape[0]

    def peer(leaf_by, sub_by):
        return (
            group_at,
            lax.rem(leaf_at + leaf_by, n_leaf),
            lax.rem(sub_at + sub_by, n_sub),
        )

    barrier = pltpu.get_barrier_semaphore()

    def greet(k, carry):
        pl.semaphore_signal(barrier, inc=1, device_id=peer(k // n_sub, k % n_sub), device_id_type=MESH)
        return carry

    lax.fori_loop(1, devices, greet, 0)
    for s in range(n_sub):
        for n in range(count):
            for part in range(2):
                mir_send[s, part, n] = pack(
                    mir_ref[n, part * leaves:(part + 1) * leaves, s * share:(s + 1) * share]
                )
    pl.semaphore_wait(barrier, devices - 1)

    def copy(src, dst, sem, leaf_by, sub_by):
        return pltpu.make_async_remote_copy(
            src_ref=src, dst_ref=dst, send_sem=send_sem.at[sem], recv_sem=recv_sem.at[sem],
            device_id=peer(leaf_by, sub_by), device_id_type=MESH,
        )

    copies = []
    for s in range(n_sub):
        to = lax.rem(sub_at + s, n_sub)
        copies.append(copy(mir_send.at[to, 1], mir_back.at[s], s, 1, s))
        copies[-1].start()
    for s in range(1, n_sub):
        to = lax.rem(sub_at + s, n_sub)
        copies.append(copy(mir_send.at[to, 0], mir_own.at[s], n_sub + s, 0, s))
        copies[-1].start()
    total = [pack(fwd_ref[n]) + mir_send[sub_at, 0, n] for n in range(count)]
    for c in copies:
        c.wait()
    for n in range(count):
        for s in range(1, n_sub):
            total[n] += mir_own[s, n]
        for s in range(n_sub):
            total[n] += mir_back[s, n]
    occ = occ_ref[...]
    direction = dir_ref[...]
    if first:
        occ = pack(occ)
        direction = pack(direction)
        occ_out[...] = occ
    if first:
        diagonal = diag_shift + total[1] / voxels
        residual = direction
        field = jnp.zeros_like(direction)
        diag_out[...] = diagonal
    else:
        diagonal = diag_ref[...]
        residual = res_ref[...]
        field = x_ref[...]
    image = diagonal * direction + occ * total[0] / voxels
    sums = (residual * residual, direction * image, residual * image, image * image)
    for i, term in enumerate(sums):
        scalars[0, i:i + 1, :] = jnp.sum(term, axis=0, keepdims=True)

    def tell(k, carry):
        copy(scalars.at[0], scalars.at[k], 4 * n_sub, k // n_sub, k % n_sub).start()
        return carry

    lax.fori_loop(1, devices, tell, 0)
    copies = []
    if not last:
        img_own[0] = occ * image
        for s in range(n_sub):
            copies.append(copy(img_own.at[0], img_ahead.at[s], 2 * n_sub + s, n_leaf - 1, s))
            copies[-1].start()
        for s in range(1, n_sub):
            copies.append(copy(img_own.at[0], img_own.at[s], 3 * n_sub + s, 0, s))
            copies[-1].start()
    everyone = copy(scalars.at[1:], scalars.at[1:], 4 * n_sub, 1, 0)
    everyone.wait()
    sums = jnp.sum(scalars[...], axis=0)
    sums = jnp.sum(sums, axis=1, keepdims=True)
    rr, dq, rq, qq = [sums[i:i + 1] for i in range(4)]
    step = rr / dq
    new = rr - 2.0 * step * rq + step * step * qq
    beta = new / rr
    field = field + step * direction
    residual = residual - step * image
    if last:
        x_out[...] = unpack(field, share)
        res_out[...] = unpack(residual, share)
        return
    x_out[...] = field
    res_out[...] = residual
    direction = residual + beta * direction
    dir_out[...] = direction
    u_out[...] = unpack(occ * direction, share)
    for c in copies:
        c.wait()
    if first:
        win_dir_ref = win_res_ref = window_ref
    for part, held in enumerate((img_own, img_ahead)):
        image_window = jnp.concatenate(
            [unpack(held[lax.rem(sub_at - s + n_sub, n_sub)], share) for s in range(n_sub)], axis=1
        )
        rows = slice(part * leaves, (part + 1) * leaves)
        res_window = win_res_ref[rows, :] - step * image_window
        win_res_out[rows, :] = res_window
        win_dir_out[rows, :] = res_window + beta * win_dir_ref[rows, :]


def update(first, last, collective_id, args):
    n_leaf, n_sub = lax.axis_size("leaf"), lax.axis_size("sub")
    count = 2 if first else 1
    leaves, share = args[0].shape[1:]
    voxels = share * n_sub
    shape = packed_shape(leaves, share)
    packed = jax.ShapeDtypeStruct(shape, jnp.float32)
    own = jax.ShapeDtypeStruct((leaves, share), jnp.float32)
    window = jax.ShapeDtypeStruct((2 * leaves, voxels), jnp.float32)
    out_shape = (own, own) if last else (packed, packed, packed, own, window, window)
    if first:
        out_shape = out_shape + (packed, packed)
    vmem = pl.BlockSpec(memory_space=pltpu.VMEM)
    return pl.pallas_call(
        functools.partial(update_kernel, first, last, n_leaf, n_sub),
        out_shape=out_shape,
        in_specs=[vmem] * len(args),
        out_specs=(vmem,) * len(out_shape),
        scratch_shapes=[
            pltpu.VMEM((n_sub, 2, count) + shape, jnp.float32),
            pltpu.VMEM((n_sub, count) + shape, jnp.float32),
            pltpu.VMEM((n_sub, count) + shape, jnp.float32),
            pltpu.VMEM((n_sub,) + shape, jnp.float32),
            pltpu.VMEM((n_sub,) + shape, jnp.float32),
            pltpu.VMEM((n_leaf * n_sub, 4, shape[1]), jnp.float32),
            pltpu.SemaphoreType.DMA((4 * n_sub + 1,)),
            pltpu.SemaphoreType.DMA((4 * n_sub + 1,)),
        ],
        compiler_params=pltpu.CompilerParams(
            collective_id=collective_id, has_side_effects=True, vmem_limit_bytes=VMEM_LIMIT
        ),
    )(*args)


def body(features, occupancy, offsets, counts, right_side):
    leaves, share = right_side.shape
    n_sub = lax.axis_size("sub")
    voxels = share * n_sub
    feat = features.shape[1] * n_sub // voxels
    occ = occupancy.astype(jnp.float32)
    masked = occ * right_side
    part = feat // n_sub
    slab = features.reshape((leaves, part, voxels)).reshape((leaves * part, voxels))
    own_slabs, ahead_slabs, window, codes = gather_all(slab, masked, offsets, counts)
    col_feat = jnp.concatenate([own_slabs, ahead_slabs]).reshape((2, n_sub, leaves, part, voxels))
    col_feat = col_feat.transpose((0, 2, 1, 3, 4)).reshape((2 * leaves, feat, voxels))
    scale = 1.0 / (2.0 * feat)
    col_w = jnp.exp(-scale * jnp.sum(jnp.square(col_feat.astype(jnp.float32)), axis=1))
    start = lax.axis_index("sub") * share
    own_rows = lax.dynamic_slice_in_dim(col_feat[:leaves], start, share, 2)
    row_w = lax.dynamic_slice_in_dim(col_w[:leaves], start, share, 1)
    row_feat = own_rows.transpose((0, 2, 1)) * jnp.bfloat16(2.0 * scale)
    feats = (row_feat, col_feat, row_w, col_w)

    fwd, mir = apply_blocks(True, codes, feats, masked, window)
    x, res, direction, u, win_dir, win_res, diagonal, occ = update(
        True, False, 0, (fwd, mir, occ, right_side, window)
    )
    for it in range(1, ITERS):
        fwd, mir = apply_blocks(False, codes, feats, u, win_dir)
        args = (fwd, mir, occ, direction, diagonal, x, res)
        if it == ITERS - 1:
            x, res = update(False, True, it, args)
        else:
            x, res, direction, u, win_dir, win_res = update(
                False, False, it, args + (win_dir, win_res)
            )
    return x, res


def solution(mesh):
    in_specs = (
        P(("groups", "leaf"), "sub"),
        P(("groups", "leaf"), "sub"),
        P(("groups", "leaf"), None),
        P(("groups", "leaf")),
        P(("groups", "leaf"), "sub"),
    )
    out_specs = (P(("groups", "leaf"), "sub"), P(("groups", "leaf"), "sub"))
    return jax.shard_map(body, mesh=mesh, in_specs=in_specs, out_specs=out_specs, check_vma=False)
```

```python
import functools

import jax
import jax.numpy as jnp
from jax import lax
from jax.experimental import pallas as pl
from jax.experimental.pallas import tpu as pltpu
from jax.sharding import PartitionSpec as P

ITERS = 3
GROUP = 32
LANES = 128
VMEM_LIMIT = 48 * 1024 * 1024
diag_shift = 0.25
MESH = pl.DeviceIdType.MESH


def pack(x):
    k = max(1, LANES // x.shape[1])
    rows = x.shape[0] // k
    return jnp.concatenate([x[i * rows:(i + 1) * rows] for i in range(k)], axis=1)


def unpack(x, share):
    return jnp.concatenate([x[:, i:i + share] for i in range(0, x.shape[1], share)], axis=0)


def packed_shape(leaves, share):
    k = max(1, LANES // share)
    return (leaves // k, share * k)


def apply_kernel(with_ones, codes_ref, row_ref, col_ref, row_w_ref, col_w_ref, u_ref, v_ref,
                 fwd_ref, mir_ref, u_wide, v_scaled, fwd_acc, mir_acc):
    leaves, share = u_ref.shape
    voxels = v_ref.shape[1]
    count = fwd_ref.shape[0]
    row_w = row_w_ref[...]
    col_w = col_w_ref[...]
    u_wide[0] = jnp.broadcast_to((u_ref[...] * row_w)[:, :, None], u_wide.shape[1:])
    v_scaled[0] = v_ref[...] * col_w
    if with_ones:
        u_wide[1] = jnp.broadcast_to(row_w[:, :, None], u_wide.shape[1:])
        v_scaled[1] = col_w
    fwd_acc[...] = jnp.zeros_like(fwd_acc)
    mir_acc[...] = jnp.zeros_like(mir_acc)

    def fold_lanes(x):
        return sum(x[:, i:i + LANES] for i in range(0, voxels, LANES))

    def fold_rows(x):
        return sum(x[i:i + 8, :] for i in range(0, share, 8))

    def group(g, carry):
        marks, blocks = [], []
        for i in range(GROUP):
            at = g * GROUP + i
            marks.append((codes_ref[0, at], codes_ref[1, at], codes_ref[2, at]))
        for row, col, mir in marks:
            blocks.append(jnp.exp(jnp.dot(
                row_ref[jnp.minimum(row, leaves - 1)], col_ref[col],
                preferred_element_type=jnp.float32,
            )))
        for (row, col, mir), block in zip(marks, blocks):
            row_read = jnp.minimum(row, leaves - 1)
            for n in range(count):
                wide = jnp.concatenate([u_wide[n, row_read]] * (voxels // LANES), axis=1)
                fwd_acc[n, row] += fold_lanes(block * v_scaled[n, pl.ds(col, 1), :])
                mir_acc[n, mir] += fold_rows(block * wide)
        return carry

    lax.fori_loop(0, codes_ref[3, 0], group, 0)
    for n in range(count):
        fwd_ref[n] = jnp.sum(fwd_acc[n, :leaves], axis=-1) * row_w
        mir_ref[n] = jnp.sum(mir_acc[n, :2 * leaves], axis=1) * col_w


def apply_blocks(with_ones, codes, feats, u, v):
    leaves, share = u.shape
    voxels = v.shape[1]
    count = 2 if with_ones else 1
    smem = pl.BlockSpec(memory_space=pltpu.SMEM)
    vmem = pl.BlockSpec(memory_space=pltpu.VMEM)
    return pl.pallas_call(
        functools.partial(apply_kernel, with_ones),
        out_shape=(
            jax.ShapeDtypeStruct((count, leaves, share), jnp.float32),
            jax.ShapeDtypeStruct((count, 2 * leaves, voxels), jnp.float32),
        ),
        in_specs=[smem] + [vmem] * 6,
        out_specs=(vmem, vmem),
        scratch_shapes=[
            pltpu.VMEM((count, leaves, share, LANES), jnp.float32),
            pltpu.VMEM((count, 2 * leaves, voxels), jnp.float32),
            pltpu.VMEM((count, leaves + 1, share, LANES), jnp.float32),
            pltpu.VMEM((count, 2 * leaves + 1, 8, voxels), jnp.float32),
        ],
        compiler_params=pltpu.CompilerParams(vmem_limit_bytes=VMEM_LIMIT),
    )(codes, *feats, u, v)


def used_blocks(offsets, counts, leaf_at, total_leaves, width):
    leaves, slots = offsets.shape
    row = lax.broadcasted_iota(jnp.int32, (leaves, 1), 0)
    place = lax.broadcasted_iota(jnp.int32, (leaves, width), 1)
    targets, used = [row], [jnp.ones((leaves, 1), jnp.int32)]
    for j in range(slots):
        target = row + offsets[:, j:j + 1]
        fits = (counts > j) & (target + leaf_at * leaves < total_leaves)
        targets.append(target)
        used.append(fits.astype(jnp.int32))
    row_count = sum(used).astype(jnp.float32)
    earlier = (
        lax.broadcasted_iota(jnp.int32, (leaves, leaves), 1)
        < lax.broadcasted_iota(jnp.int32, (leaves, leaves), 0)
    ).astype(jnp.float32)
    at = jnp.dot(
        earlier, jnp.broadcast_to(row_count, (leaves, LANES)), preferred_element_type=jnp.float32
    )[:, :1].astype(jnp.int32)
    rows = jnp.zeros((leaves, width), jnp.int32)
    cols = jnp.zeros((leaves, width), jnp.int32)
    for target, use in zip(targets, used):
        hit = (place == at) & (use > 0)
        rows = rows + jnp.where(hit, row - leaves, 0)
        cols = cols + jnp.where(hit, target - leaves, 0)
        at = at + use
    rows = jnp.sum(rows, axis=0, keepdims=True) + leaves
    cols = jnp.sum(cols, axis=0, keepdims=True) + leaves
    turns = (jnp.sum(row_count, axis=0, keepdims=True).astype(jnp.int32) + (GROUP - 1)) // GROUP
    mirrors = jnp.where(rows == cols, 2 * leaves, cols)
    return jnp.concatenate([rows, cols, mirrors, jnp.broadcast_to(turns, rows.shape)], axis=0)


def gather_kernel(n_leaf, n_sub, slab_ref, field_ref, offsets_ref, counts_ref,
                  own_out, ahead_out, window_out, codes_out,
                  field_own, field_ahead, send_sem, recv_sem, field_send, field_recv):
    group_at = lax.axis_index("groups")
    leaf_at = lax.axis_index("leaf")
    sub_at = lax.axis_index("sub")
    inner = 2 if n_sub % 2 == 0 else 1
    n_out = n_sub // inner
    out_at = sub_at // inner
    in_at = sub_at % inner
    leaves, share = field_ref.shape
    behind = lax.rem(leaf_at + n_leaf - 1, n_leaf)
    devices = n_leaf * n_sub

    barrier = pltpu.get_barrier_semaphore()

    def greet(k, carry):
        to = (
            group_at,
            lax.rem(leaf_at + k // n_sub, n_leaf),
            lax.rem(sub_at + k % n_sub, n_sub),
        )
        pl.semaphore_signal(barrier, inc=1, device_id=to, device_id_type=MESH)
        return carry

    lax.fori_loop(1, devices, greet, 0)
    field_own[0] = pack(field_ref[...])
    pl.semaphore_wait(barrier, devices - 1)

    sent = []

    def send(src, dst, slot, leaf, sub):
        c = pltpu.make_async_remote_copy(
            src_ref=src, dst_ref=dst, send_sem=send_sem.at[len(sent)], recv_sem=recv_sem.at[slot],
            device_id=(group_at, leaf, sub), device_id_type=MESH,
        )
        c.start()
        sent.append(c)

    half = slab_ref.shape[0] // 2

    def arrived(dst, slot, src=slab_ref):
        pltpu.make_async_remote_copy(
            src_ref=src, dst_ref=dst, send_sem=send_sem.at[0], recv_sem=recv_sem.at[slot],
            device_id=(group_at, leaf_at, sub_at), device_id_type=MESH,
        ).wait_recv()

    def sub_of(outer_by, other):
        return lax.rem(out_at + outer_by, n_out) * inner + (inner - 1 - in_at if other else in_at)

    partner = sub_of(0, True)
    send(slab_ref, ahead_out.at[sub_at], n_sub + sub_at, behind, sub_at)
    for d in range(1, n_out):
        send(slab_ref, own_out.at[sub_at], sub_at, leaf_at, sub_of(d, False))
    if inner == 2:
        send(slab_ref, own_out.at[sub_at], sub_at, leaf_at, partner)
    field_copies = []
    for s in range(n_sub):
        to = lax.rem(sub_at + s, n_sub)
        field_copies.append(pltpu.make_async_remote_copy(
            src_ref=field_own.at[0], dst_ref=field_ahead.at[s],
            send_sem=field_send.at[s], recv_sem=field_recv.at[s],
            device_id=(group_at, behind, to), device_id_type=MESH,
        ))
        if s:
            field_copies.append(pltpu.make_async_remote_copy(
                src_ref=field_own.at[0], dst_ref=field_own.at[s],
                send_sem=field_send.at[n_sub + s], recv_sem=field_recv.at[n_sub + s],
                device_id=(group_at, leaf_at, to), device_id_type=MESH,
            ))
    for c in field_copies:
        c.start()
    own_out[sub_at] = slab_ref[...]
    codes_out[...] = used_blocks(
        offsets_ref[...], counts_ref[...], leaf_at, n_leaf * leaves, codes_out.shape[1]
    )
    arrived(ahead_out.at[sub_at], n_sub + sub_at)
    low, high = pl.ds(0, half), pl.ds(half, half)
    for d in range(1, n_out):
        send(ahead_out.at[sub_at, low], ahead_out.at[sub_at, low], n_sub + sub_at, leaf_at, sub_of(d, False))
    for d in range(1, n_out):
        slot = sub_of(n_out - d, False)
        arrived(own_out.at[slot], slot)
        send(own_out.at[slot, high], ahead_out.at[slot, high], 2 * n_sub + slot, behind, sub_at)
        if inner == 2:
            send(own_out.at[slot], own_out.at[slot], slot, leaf_at, partner)
    if inner == 2:
        send(ahead_out.at[sub_at], ahead_out.at[sub_at], n_sub + sub_at, leaf_at, partner)
    for d in range(1, n_out):
        slot = sub_of(n_out - d, False)
        arrived(ahead_out.at[slot, low], n_sub + slot, slab_ref.at[low])
        arrived(ahead_out.at[slot, high], 2 * n_sub + slot, slab_ref.at[high])
        if inner == 2:
            send(ahead_out.at[slot], ahead_out.at[slot], n_sub + slot, leaf_at, partner)
    for c in field_copies:
        c.wait()
    for part, held in enumerate((field_own, field_ahead)):
        window_out[part * leaves:(part + 1) * leaves, :] = jnp.concatenate(
            [unpack(held[lax.rem(sub_at - s + n_sub, n_sub)], share) for s in range(n_sub)], axis=1
        )
    if inner == 2:
        for base, out in ((0, own_out), (n_sub, ahead_out)):
            for d in range(n_out):
                slot = sub_of(n_out - d, True)
                arrived(out.at[slot], base + slot)
    for c in sent:
        c.wait_send()


def gather_all(slab, field, offsets, counts):
    n_leaf, n_sub = lax.axis_size("leaf"), lax.axis_size("sub")
    leaves, share = field.shape
    vmem = pl.BlockSpec(memory_space=pltpu.VMEM)
    slabs = jax.ShapeDtypeStruct((n_sub,) + slab.shape, slab.dtype)
    length = -(-leaves * (offsets.shape[1] + 1) // LANES) * LANES
    return pl.pallas_call(
        functools.partial(gather_kernel, n_leaf, n_sub),
        out_shape=(slabs, slabs, jax.ShapeDtypeStruct((2 * leaves, share * n_sub), jnp.float32),
                   jax.ShapeDtypeStruct((4, length), jnp.int32)),
        in_specs=[vmem] * 4,
        out_specs=(vmem,) * 4,
        scratch_shapes=[
            pltpu.VMEM((n_sub,) + packed_shape(leaves, share), jnp.float32),
            pltpu.VMEM((n_sub,) + packed_shape(leaves, share), jnp.float32),
            pltpu.SemaphoreType.DMA((3 * n_sub + 2,)),
            pltpu.SemaphoreType.DMA((3 * n_sub,)),
            pltpu.SemaphoreType.DMA((2 * n_sub,)),
            pltpu.SemaphoreType.DMA((2 * n_sub,)),
        ],
        compiler_params=pltpu.CompilerParams(
            collective_id=ITERS, has_side_effects=True, vmem_limit_bytes=VMEM_LIMIT
        ),
    )(slab, field, offsets, counts[:, None])


def update_kernel(first, last, n_leaf, n_sub, *refs):
    refs = list(refs)
    fwd_ref, mir_ref, occ_ref, dir_ref = refs[:4]
    del refs[:4]
    if first:
        window_ref = refs.pop(0)
        out_refs = refs[:8]
        del refs[:8]
        x_out, res_out, dir_out, u_out, win_dir_out, win_res_out, diag_out, occ_out = out_refs
    else:
        diag_ref, x_ref, res_ref = refs[:3]
        del refs[:3]
        if last:
            x_out, res_out = refs[:2]
            del refs[:2]
        else:
            win_dir_ref, win_res_ref = refs[:2]
            x_out, res_out, dir_out, u_out, win_dir_out, win_res_out = refs[2:8]
            del refs[:8]
    mir_send, mir_own, mir_back, img_own, img_ahead, scalars, send_sem, recv_sem = refs

    group_at = lax.axis_index("groups")
    leaf_at = lax.axis_index("leaf")
    sub_at = lax.axis_index("sub")
    devices = n_leaf * n_sub
    leaves, share = fwd_ref.shape[1:]
    voxels = share * n_sub
    count = fwd_ref.shape[0]

    def peer(leaf_by, sub_by):
        return (
            group_at,
            lax.rem(leaf_at + leaf_by, n_leaf),
            lax.rem(sub_at + sub_by, n_sub),
        )

    barrier = pltpu.get_barrier_semaphore()

    def greet(k, carry):
        pl.semaphore_signal(barrier, inc=1, device_id=peer(k // n_sub, k % n_sub), device_id_type=MESH)
        return carry

    lax.fori_loop(1, devices, greet, 0)
    for s in range(n_sub):
        for n in range(count):
            for part in range(2):
                mir_send[s, part, n] = pack(
                    mir_ref[n, part * leaves:(part + 1) * leaves, s * share:(s + 1) * share]
                )
    pl.semaphore_wait(barrier, devices - 1)

    def copy(src, dst, sem, leaf_by, sub_by):
        return pltpu.make_async_remote_copy(
            src_ref=src, dst_ref=dst, send_sem=send_sem.at[sem], recv_sem=recv_sem.at[sem],
            device_id=peer(leaf_by, sub_by), device_id_type=MESH,
        )

    copies = []
    for s in range(n_sub):
        to = lax.rem(sub_at + s, n_sub)
        copies.append(copy(mir_send.at[to, 1], mir_back.at[s], s, 1, s))
        copies[-1].start()
    for s in range(1, n_sub):
        to = lax.rem(sub_at + s, n_sub)
        copies.append(copy(mir_send.at[to, 0], mir_own.at[s], n_sub + s, 0, s))
        copies[-1].start()
    total = [pack(fwd_ref[n]) + mir_send[sub_at, 0, n] for n in range(count)]
    for c in copies:
        c.wait()
    for n in range(count):
        for s in range(1, n_sub):
            total[n] += mir_own[s, n]
        for s in range(n_sub):
            total[n] += mir_back[s, n]
    occ = occ_ref[...]
    direction = dir_ref[...]
    if first:
        occ = pack(occ)
        direction = pack(direction)
        occ_out[...] = occ
    if first:
        diagonal = diag_shift + total[1] / voxels
        residual = direction
        field = jnp.zeros_like(direction)
        diag_out[...] = diagonal
    else:
        diagonal = diag_ref[...]
        residual = res_ref[...]
        field = x_ref[...]
    image = diagonal * direction + occ * total[0] / voxels
    sums = (residual * residual, direction * image, residual * image, image * image)
    for i, term in enumerate(sums):
        scalars[0, i:i + 1, :] = jnp.sum(term, axis=0, keepdims=True)

    def tell(k, carry):
        copy(scalars.at[0], scalars.at[k], 4 * n_sub, k // n_sub, k % n_sub).start()
        return carry

    lax.fori_loop(1, devices, tell, 0)
    copies = []
    if not last:
        img_own[0] = occ * image
        for s in range(n_sub):
            copies.append(copy(img_own.at[0], img_ahead.at[s], 2 * n_sub + s, n_leaf - 1, s))
            copies[-1].start()
        for s in range(1, n_sub):
            copies.append(copy(img_own.at[0], img_own.at[s], 3 * n_sub + s, 0, s))
            copies[-1].start()
    everyone = copy(scalars.at[1:], scalars.at[1:], 4 * n_sub, 1, 0)
    everyone.wait()
    sums = jnp.sum(scalars[...], axis=0)
    sums = jnp.sum(sums, axis=1, keepdims=True)
    rr, dq, rq, qq = [sums[i:i + 1] for i in range(4)]
    step = rr / dq
    new = rr - 2.0 * step * rq + step * step * qq
    beta = new / rr
    field = field + step * direction
    residual = residual - step * image
    if last:
        x_out[...] = unpack(field, share)
        res_out[...] = unpack(residual, share)
        return
    x_out[...] = field
    res_out[...] = residual
    direction = residual + beta * direction
    dir_out[...] = direction
    u_out[...] = unpack(occ * direction, share)
    for c in copies:
        c.wait()
    if first:
        win_dir_ref = win_res_ref = window_ref
    for part, held in enumerate((img_own, img_ahead)):
        image_window = jnp.concatenate(
            [unpack(held[lax.rem(sub_at - s + n_sub, n_sub)], share) for s in range(n_sub)], axis=1
        )
        rows = slice(part * leaves, (part + 1) * leaves)
        res_window = win_res_ref[rows, :] - step * image_window
        win_res_out[rows, :] = res_window
        win_dir_out[rows, :] = res_window + beta * win_dir_ref[rows, :]


def update(first, last, collective_id, args):
    n_leaf, n_sub = lax.axis_size("leaf"), lax.axis_size("sub")
    count = 2 if first else 1
    leaves, share = args[0].shape[1:]
    voxels = share * n_sub
    shape = packed_shape(leaves, share)
    packed = jax.ShapeDtypeStruct(shape, jnp.float32)
    own = jax.ShapeDtypeStruct((leaves, share), jnp.float32)
    window = jax.ShapeDtypeStruct((2 * leaves, voxels), jnp.float32)
    out_shape = (own, own) if last else (packed, packed, packed, own, window, window)
    if first:
        out_shape = out_shape + (packed, packed)
    vmem = pl.BlockSpec(memory_space=pltpu.VMEM)
    return pl.pallas_call(
        functools.partial(update_kernel, first, last, n_leaf, n_sub),
        out_shape=out_shape,
        in_specs=[vmem] * len(args),
        out_specs=(vmem,) * len(out_shape),
        scratch_shapes=[
            pltpu.VMEM((n_sub, 2, count) + shape, jnp.float32),
            pltpu.VMEM((n_sub, count) + shape, jnp.float32),
            pltpu.VMEM((n_sub, count) + shape, jnp.float32),
            pltpu.VMEM((n_sub,) + shape, jnp.float32),
            pltpu.VMEM((n_sub,) + shape, jnp.float32),
            pltpu.VMEM((n_leaf * n_sub, 4, shape[1]), jnp.float32),
            pltpu.SemaphoreType.DMA((4 * n_sub + 1,)),
            pltpu.SemaphoreType.DMA((4 * n_sub + 1,)),
        ],
        compiler_params=pltpu.CompilerParams(
            collective_id=collective_id, has_side_effects=True, vmem_limit_bytes=VMEM_LIMIT
        ),
    )(*args)


def body(features, occupancy, offsets, counts, right_side):
    leaves, share = right_side.shape
    n_sub = lax.axis_size("sub")
    voxels = share * n_sub
    feat = features.shape[1] * n_sub // voxels
    occ = occupancy.astype(jnp.float32)
    masked = occ * right_side
    part = feat // n_sub
    slab = features.reshape((leaves, part, voxels)).reshape((leaves * part, voxels))
    own_slabs, ahead_slabs, window, codes = gather_all(slab, masked, offsets, counts)
    col_feat = jnp.concatenate([own_slabs, ahead_slabs]).reshape((2, n_sub, leaves, part, voxels))
    col_feat = col_feat.transpose((0, 2, 1, 3, 4)).reshape((2 * leaves, feat, voxels))
    scale = 1.0 / (2.0 * feat)
    col_w = jnp.exp(-scale * jnp.sum(jnp.square(col_feat.astype(jnp.float32)), axis=1))
    start = lax.axis_index("sub") * share
    own_rows = lax.dynamic_slice_in_dim(col_feat[:leaves], start, share, 2)
    row_w = lax.dynamic_slice_in_dim(col_w[:leaves], start, share, 1)
    row_feat = own_rows.transpose((0, 2, 1)) * jnp.bfloat16(2.0 * scale)
    feats = (row_feat, col_feat, row_w, col_w)

    fwd, mir = apply_blocks(True, codes, feats, masked, window)
    x, res, direction, u, win_dir, win_res, diagonal, occ = update(
        True, False, 0, (fwd, mir, occ, right_side, window)
    )
    for it in range(1, ITERS):
        fwd, mir = apply_blocks(False, codes, feats, u, win_dir)
        args = (fwd, mir, occ, direction, diagonal, x, res)
        if it == ITERS - 1:
            x, res = update(False, True, it, args)
        else:
            x, res, direction, u, win_dir, win_res = update(
                False, False, it, args + (win_dir, win_res)
            )
    return x, res


def solution(mesh):
    in_specs = (
        P(("groups", "leaf"), "sub"),
        P(("groups", "leaf"), "sub"),
        P(("groups", "leaf"), None),
        P(("groups", "leaf")),
        P(("groups", "leaf"), "sub"),
    )
    out_specs = (P(("groups", "leaf"), "sub"), P(("groups", "leaf"), "sub"))
    return jax.shard_map(body, mesh=mesh, in_specs=in_specs, out_specs=out_specs, check_vma=False)
```
